32 devices in a mesh: tm: 4 (over z), src: 4 (over x, core), rcv: 2 (over y).
Axes of the slice: x: 2, y: 2, z: 4, core: 2. Of those that a mesh axis runs over, the one named last changes fastest.
Arguments:
- src_real: bfloat16 [5, 1024, 2048], P(None, 'tm', 'src'), may hold values from -6 to 6
- src_imag: bfloat16 [5, 1024, 2048], P(None, 'tm', 'src'), may hold values from -6 to 6
- rcv_real: bfloat16 [5, 1024, 2048], P(None, 'tm', 'rcv'), may hold values from -6 to 6
- rcv_imag: bfloat16 [5, 1024, 2048], P(None, 'tm', 'rcv'), may hold values from -6 to 6
- src_pos: float32 [2048], replicated, may hold values from -1 to 1
- rcv_pos: float32 [2048], replicated, may hold values from -1 to 1
- freqs: float32 [5], replicated, may hold values from 60 to 120
Outputs:
- beam: float32 [2048, 2, 5, 2048], P('src', None, None, ('tm', 'rcv'))
The draws below stay inside these ranges and needn't reach their ends.
All inputs are finite; a program needn't handle non-finite values.
Results may differ from the reference program's by a relative error of at most 0.0052.
Values may be sent and summed in bfloat16 or wider, within the bound.
No kernel may reach another device: no remote copies, remote signals or barrier semaphores. Data moves between devices by JAX's collectives and lax.ppermute only.
A program may use at most 128 MiB of HBM per device.

```python
import math
import jax
import jax.numpy as jnp

BINS = 5
SRC_ST = 2048
RCV_ST = 2048
SRC_SL = 2048
RCV_SL = 2048
WINDOWS = 1024


def steps_of(stream_key, extent, pieces, least, largest):
    loudness, own = 1.0, jax.random.fold_in(stream_key, 6)
    for dim, blocks in pieces:
        steps = jnp.exp(jax.random.uniform(jax.random.fold_in(own, dim), (blocks,), jnp.float32, least / len(pieces), largest / len(pieces)))
        loudness = loudness * jnp.repeat(steps, extent[dim] // blocks).reshape([-1 if axis == dim else 1 for axis in range(len(extent))])
    return loudness


def noise(rng, extent, deviation, most, split=(), held_as=jnp.bfloat16):
    array = jax.random.normal(rng, extent, jnp.float32) * deviation
    if len(split) > 0:
        array = steps_of(rng, extent, split, -0.22, 0.18) * array
    return jnp.clip(array, min=-most, max=most).astype(held_as)


def setup_inputs(seed: int = 0) -> dict:
    keys = jax.random.split(jax.random.key(seed), 8)
    return {
        "src_real": noise(keys[0], (BINS, WINDOWS, SRC_ST), 1.0, 6.0, ((1, 4), (2, 4))),
        "src_imag": noise(keys[1], (BINS, WINDOWS, SRC_ST), 1.0, 6.0, ((1, 4), (2, 4))),
        "rcv_real": noise(keys[2], (BINS, WINDOWS, RCV_ST), 1.0, 6.0, ((1, 4), (2, 2))),
        "rcv_imag": noise(keys[3], (BINS, WINDOWS, RCV_ST), 1.0, 6.0, ((1, 4), (2, 2))),
        "src_pos": jnp.clip(jax.random.uniform(keys[4], (SRC_ST,), jnp.float32, -1.0, 1.0), -1.0, 1.0),
        "rcv_pos": jnp.clip(jax.random.uniform(keys[5], (RCV_ST,), jnp.float32, -1.0, 1.0), -1.0, 1.0),
        "freqs": jnp.clip(jnp.exp(jax.random.uniform(keys[6], (BINS,), jnp.float32, math.log(60.0), math.log(120.0))), 60.0, 120.0),
    }


TWO_PI = 6.283185307179586

def grid_points(first, count, total):
    index = (first + jnp.arange(count, dtype=jnp.int32)).astype(jnp.float32)
    return (2.0 * index + 1.0) / total - 1.0

def phases(freqs, slowness, positions):
    return (TWO_PI * freqs)[:, None, None] * slowness[None, :, None] * positions[None, None, :]

def product(form, first, second):
    return jnp.einsum(form, first.astype(jnp.float32), second.astype(jnp.float32))

def reference(src_real, src_imag, rcv_real, rcv_imag, src_pos, rcv_pos, freqs):
    cross_real = (product('fwa,fwb->fab', src_real, rcv_real) + product('fwa,fwb->fab', src_imag, rcv_imag)).astype(jnp.bfloat16)
    cross_imag = (product('fwa,fwb->fab', src_imag, rcv_real) - product('fwa,fwb->fab', src_real, rcv_imag)).astype(jnp.bfloat16)
    angle_rcv = phases(freqs, grid_points(0, RCV_SL, RCV_SL), rcv_pos)
    rsteer_real = jnp.cos(angle_rcv).astype(jnp.bfloat16)
    rsteer_imag = jnp.sin(angle_rcv).astype(jnp.bfloat16)
    focus_scale = 1.0 / jnp.sqrt(jnp.float32(WINDOWS * RCV_ST))
    focus_real = product('fab,fqb->faq', cross_real, rsteer_real) - product('fab,fqb->faq', cross_imag, rsteer_imag)
    focus_imag = product('fab,fqb->faq', cross_real, rsteer_imag) + product('fab,fqb->faq', cross_imag, rsteer_real)
    focus_real = (focus_real * focus_scale).astype(jnp.bfloat16)
    focus_imag = (focus_imag * focus_scale).astype(jnp.bfloat16)
    angle_src = phases(freqs, grid_points(0, SRC_SL, SRC_SL), src_pos)
    ssteer_real = jnp.cos(angle_src).astype(jnp.bfloat16)
    ssteer_imag = (-jnp.sin(angle_src)).astype(jnp.bfloat16)
    beam_real = product('fpa,faq->pfq', ssteer_real, focus_real) - product('fpa,faq->pfq', ssteer_imag, focus_imag)
    beam_imag = product('fpa,faq->pfq', ssteer_real, focus_imag) + product('fpa,faq->pfq', ssteer_imag, focus_real)
    beam_scale = 1.0 / jnp.sqrt(jnp.float32(SRC_ST))
    return jnp.stack([beam_real, beam_imag], 1) * beam_scale
```

```python
import jax
import jax.numpy as jnp
from jax import lax
from jax.sharding import PartitionSpec as P

SRC_ST = 2048
RCV_ST = 2048
SRC_SL = 2048
RCV_SL = 2048


TWO_PI = 6.283185307179586


def grid_points(first, count, total):
    index = (first + jnp.arange(count, dtype=jnp.int32)).astype(jnp.float32)
    return (2.0 * index + 1.0) / total - 1.0


def phases(freqs, slowness, positions):
    return (TWO_PI * freqs)[:, None, None] * slowness[None, :, None] * positions[None, None, :]


def mixed(form, first, second):
    return jnp.einsum(form, first, second, preferred_element_type=jnp.float32)


def receiver_fold(freqs, slow_rcv, locate, piece, start):
    part_real, part_imag = piece
    where = locate(start, part_real.shape[2])
    angle = phases(freqs, slow_rcv, where)
    steer_real = jnp.cos(angle).astype(jnp.bfloat16)
    steer_imag = jnp.sin(angle).astype(jnp.bfloat16)
    new_real = mixed("fab,fqb->faq", part_real, steer_real) - mixed(
        "fab,fqb->faq", part_imag, steer_imag
    )
    new_imag = mixed("fab,fqb->faq", part_real, steer_imag) + mixed(
        "fab,fqb->faq", part_imag, steer_real
    )
    return (new_real, new_imag)


def source_terms(freqs, slow_src, positions, focus_real, focus_imag):
    angle = phases(freqs, slow_src, positions)
    steer_real = jnp.cos(angle).astype(jnp.bfloat16)
    steer_imag = (-jnp.sin(angle)).astype(jnp.bfloat16)
    term_real = mixed("fpa,faq->pfq", steer_real, focus_real) - mixed(
        "fpa,faq->pfq", steer_imag, focus_imag
    )
    term_imag = mixed("fpa,faq->pfq", steer_real, focus_imag) + mixed(
        "fpa,faq->pfq", steer_imag, focus_real
    )
    return (term_real, term_imag)


def shards_any(src_real, src_imag, rcv_real, rcv_imag, src_pos, rcv_pos, freqs):
    n_time = lax.axis_size("tm")
    n_recv = lax.axis_size("rcv")
    n_source = lax.axis_size("src")
    src_block = src_real.shape[2]
    rcv_block = rcv_real.shape[2]
    windows = src_real.shape[1] * n_time
    q_block = RCV_SL // (n_time * n_recv)
    p_block = SRC_SL // n_source
    src_both = jnp.concatenate([src_real, src_imag], 1)
    rcv_plain = jnp.concatenate([rcv_real, rcv_imag], 1)
    rcv_turned = jnp.concatenate([-rcv_imag, rcv_real], 1)
    part_real = mixed("fwa,fwb->fab", src_both, rcv_plain)
    part_imag = mixed("fwa,fwb->fab", src_both, rcv_turned)
    q_first = (lax.axis_index("tm") * n_recv + lax.axis_index("rcv")) * q_block
    slow_rcv = grid_points(q_first, q_block, RCV_SL)
    sum_real, sum_imag = (
        lax.psum_scatter(part_real, "tm", scatter_dimension=2, tiled=True),
        lax.psum_scatter(part_imag, "tm", scatter_dimension=2, tiled=True),
    )
    sub_width = rcv_block // n_time

    def mapped(start, count):
        column = jnp.arange(count, dtype=jnp.int32)
        block = column // sub_width
        natural = block % n_recv * rcv_block + block // n_recv * sub_width + column % sub_width
        return jnp.take(rcv_pos, natural)

    cross = (sum_real.astype(jnp.bfloat16), sum_imag.astype(jnp.bfloat16))
    focus_real, focus_imag = receiver_fold(
        freqs,
        slow_rcv,
        mapped,
        (
            lax.all_gather(cross[0], ("tm", "rcv"), axis=2, tiled=True),
            lax.all_gather(cross[1], ("tm", "rcv"), axis=2, tiled=True),
        ),
        jnp.int32(0),
    )
    focus_scale = 1.0 / jnp.sqrt(jnp.float32(windows * RCV_ST))
    focus_real = (focus_real * focus_scale).astype(jnp.bfloat16)
    focus_imag = (focus_imag * focus_scale).astype(jnp.bfloat16)
    beam_scale = 1.0 / jnp.sqrt(jnp.float32(SRC_ST))
    own_pos = lax.dynamic_slice_in_dim(src_pos, lax.axis_index("src") * src_block, src_block)
    slow_src = grid_points(jnp.int32(0), p_block * lax.axis_size("src"), SRC_SL)
    term_real, term_imag = source_terms(freqs, slow_src, own_pos, focus_real, focus_imag)
    return lax.psum_scatter(
        jnp.stack([term_real, term_imag], 1) * beam_scale, "src", scatter_dimension=0, tiled=True
    )


FINE = 32
CHUNKS = 4


def waves(freq, slowness, positions):
    angle = ((TWO_PI * freq) * slowness)[:, None] * positions[None, :]
    return jnp.cos(angle), jnp.sin(angle)


def steering(freq, starts, total, positions):
    coarse = (2.0 * starts.astype(jnp.float32) + 1.0) / total - 1.0
    fine = 2.0 * jnp.arange(FINE, dtype=jnp.float32) / total
    cos_c, sin_c = waves(freq, coarse, positions)
    cos_f, sin_f = waves(freq, fine, positions)
    one = jnp.concatenate([cos_c, sin_c], 1)
    two = jnp.concatenate([-sin_c, cos_c], 1)
    by_cos = jnp.concatenate([cos_f, cos_f], 1)
    by_sin = jnp.concatenate([sin_f, sin_f], 1)
    one, two, by_cos, by_sin = lax.optimization_barrier((one, two, by_cos, by_sin))
    full = one[:, None, :] * by_cos[None] + two[:, None, :] * by_sin[None]
    return full.astype(jnp.bfloat16).reshape(starts.shape[0] * FINE, -1)


def runs(first, count):
    return first + FINE * jnp.arange(count // FINE, dtype=jnp.int32)


def bin_of(real, imag, which):
    return jnp.stack([lax.dynamic_index_in_dim(part, which, 0, False) for part in (real, imag)])


def nt(first, second):
    return lax.dot_general(first, second, (((1,), (1,)), ((), ())), preferred_element_type=jnp.float32)


def shards_plane(src_real, src_imag, rcv_real, rcv_imag, src_pos, rcv_pos, freqs):
    n_z = lax.axis_size("tm")
    bins, wide, a_block = src_real.shape
    b_block = rcv_real.shape[2]
    half_b = wide // 2
    p_block = SRC_SL // lax.axis_size("src")
    q_plane = RCV_SL // n_z
    q_block = q_plane // 2
    q_sub = q_block // lax.axis_size("src")
    z, s, y = (lax.axis_index(name) for name in ("tm", "src", "rcv"))
    x, c = s // 2, s % 2
    mine = 2 * x + y
    last = bins - 1
    core = lambda v: lax.ppermute(v, "src", [(i, i ^ 1) for i in range(4)])
    over_x = lambda v: lax.ppermute(v, "src", [(i, i ^ 2) for i in range(4)])
    over_y = lambda v: lax.ppermute(v, "rcv", [(0, 1), (1, 0)])
    over_xy = lambda v: lax.ppermute(v, ("src", "rcv"), [(i, i ^ 5) for i in range(8)])

    def all_sources(theirs, ours):
        given = over_x(bin_of(src_real, src_imag, theirs))
        own = bin_of(src_real, src_imag, ours)
        other_own, other_given = core(own), core(given)
        both = jnp.concatenate([own, given, other_own, other_given], 2)
        return jnp.concatenate(
            [jnp.concatenate([both[0], both[1]], 1), jnp.concatenate([both[1], -both[0]], 1)], 0
        )

    def all_receivers(theirs, ours):
        cut = lambda v: lax.dynamic_slice_in_dim(v, c * half_b, half_b, 1)
        given = over_y(cut(bin_of(rcv_real, rcv_imag, theirs)))
        other = core(given)
        given, other = jnp.where(c == 0, given, other), jnp.where(c == 0, other, given)
        both = jnp.concatenate([bin_of(rcv_real, rcv_imag, ours), jnp.concatenate([given, other], 1)], 2)
        return jnp.concatenate(
            [jnp.concatenate([both[0], both[1]], 1), jnp.concatenate([-both[1], both[0]], 1)], 0
        )

    x_mine = all_sources(2 * (1 - x) + y, mine)
    y_mine = all_receivers(2 * x + 1 - y, mine)
    x_last = all_sources(last, last)
    y_last = all_receivers(last, last)
    take = lambda v, block, size: lax.dynamic_slice_in_dim(v, block * size, size)
    at_src = jnp.concatenate([take(src_pos, block, a_block) for block in (s, s ^ 2, s ^ 1, s ^ 3)])
    at_rcv = jnp.concatenate([take(rcv_pos, block, b_block) for block in (y, 1 - y)])
    f_mine, f_last = lax.dynamic_index_in_dim(freqs, mine, 0, False), freqs[last]

    chunk = p_block // CHUNKS
    here, there = s * p_block, (s ^ 2) * p_block
    starts = jnp.concatenate(
        [runs(first + k * chunk, chunk) for k in range(CHUNKS) for first in (here, there)]
    )
    s_mine = steering(f_mine, starts, SRC_SL, at_src)
    s_last = steering(f_last, runs(here + y * (p_block // 2), p_block // 2), SRC_SL, at_src)
    xs_mine = nt(s_mine, x_mine).astype(jnp.bfloat16)
    xs_last = nt(s_last, x_last).astype(jnp.bfloat16)

    planes = [(z + d) % n_z for d in range(n_z)]
    r_mine = steering(
        f_mine, jnp.concatenate([runs(to * q_plane + c * q_block, q_block) for to in planes]), RCV_SL, at_rcv
    )
    r_last = steering(
        f_last,
        jnp.concatenate([runs(to * q_plane + y * q_block + s * q_sub, q_sub) for to in planes]),
        RCV_SL,
        at_rcv,
    )
    yr_mine = nt(y_mine, r_mine).astype(jnp.bfloat16)
    yr_last = nt(y_last, r_last).astype(jnp.bfloat16)

    def to_planes(v, size):
        got = [v[:, :size]]
        for d in range(1, n_z):
            part = v[:, d * size : (d + 1) * size]
            got.append(lax.ppermute(part, "tm", [(i, (i + d) % n_z) for i in range(n_z)]))
        return jnp.concatenate(got, 0)

    def chain(v):
        up, down = [v], [v]
        for d in range(1, n_z):
            up.append(lax.ppermute(up[-1], "tm", [(i, i + 1) for i in range(d - 1, n_z - 1)]))
            down.append(lax.ppermute(down[-1], "tm", [(i, i - 1) for i in range(1, n_z - d + 1)]))
        return jnp.concatenate([v] + [up[d] + down[n_z - d] for d in range(1, n_z)], 1)

    pieces = [xs_mine[2 * k * chunk : 2 * (k + 1) * chunk] for k in range(CHUNKS)]
    yr_mine = to_planes(yr_mine, q_block)
    yr_last = to_planes(yr_last, q_sub)
    pieces = [chain(piece) for piece in pieces]
    xs_last = chain(xs_last)

    def product_side(v):
        v = v.reshape(n_z, 2, wide, -1)
        real, imag = v[:, 0], v[:, 1]
        full = jnp.stack([jnp.concatenate([real, imag], 2), jnp.concatenate([-imag, real], 2)], 1)
        return full.reshape(n_z * 2 * wide, -1)

    yr_other = core(yr_mine)
    keep_mine = product_side(jnp.where(c == y, yr_mine, yr_other))
    send_mine = product_side(jnp.where(c == y, yr_other, yr_mine))
    every = lax.all_gather(yr_last, ("rcv", "src"), axis=0).reshape(2, 4, n_z * 2 * wide, q_sub)
    every = every.transpose(0, 2, 1, 3).reshape(2, n_z * 2 * wide, q_block)
    keep_last = product_side(lax.dynamic_index_in_dim(every, y, 0, False))
    send_last = product_side(lax.dynamic_index_in_dim(every, 1 - y, 0, False))

    scale = 1.0 / jnp.sqrt(jnp.float32(wide * n_z * RCV_ST)) * (1.0 / jnp.sqrt(jnp.float32(SRC_ST)))
    times = lambda one, two: jnp.dot(one, two, preferred_element_type=jnp.float32) * scale
    found = [[], [], [], []]
    for piece in pieces:
        keep, send = times(piece, keep_mine), times(piece, send_mine)
        found[0].append(keep[:chunk])
        found[1].append(over_y(send[:chunk]))
        found[2].append(over_x(keep[chunk:]))
        found[3].append(over_xy(send[chunk:]))
    found = [jnp.concatenate(parts, 0) for parts in found]
    keep, send = times(xs_last, keep_last), over_y(times(xs_last, send_last))
    low, high = jnp.where(y == 0, keep, send), jnp.where(y == 0, send, keep)
    swap = lambda bit, one, two: (jnp.where(bit == 0, one, two), jnp.where(bit == 0, two, one))
    f0, f1 = swap(y, found[0], found[1])
    f2, f3 = swap(y, found[2], found[3])
    f0, f2 = swap(x, f0, f2)
    f1, f3 = swap(x, f1, f3)
    whole = [f0, f1, f2, f3, jnp.concatenate([low, high], 0)]
    return jnp.stack([v.reshape(p_block, 2, q_block) for v in whole], 2)


def solution(mesh):
    plane = (mesh.shape["src"], mesh.shape["rcv"]) == (4, 2)
    shards = shards_plane if plane else shards_any
    in_specs = (
        P(None, "tm", "src"),
        P(None, "tm", "src"),
        P(None, "tm", "rcv"),
        P(None, "tm", "rcv"),
        P(),
        P(),
        P(),
    )
    out_specs = P("src", None, None, ("tm", "rcv"))
    return jax.shard_map(shards, mesh=mesh, in_specs=in_specs, out_specs=out_specs, check_vma=False)
```

```python
import jax
import jax.numpy as jnp
from jax import lax
from jax.experimental import pallas as pl
from jax.experimental.pallas import tpu as pltpu
from jax.sharding import PartitionSpec as P

SRC_ST = 2048
RCV_ST = 2048
SRC_SL = 2048
RCV_SL = 2048


TWO_PI = 6.283185307179586


def grid_points(first, count, total):
    index = (first + jnp.arange(count, dtype=jnp.int32)).astype(jnp.float32)
    return (2.0 * index + 1.0) / total - 1.0


def phases(freqs, slowness, positions):
    return (TWO_PI * freqs)[:, None, None] * slowness[None, :, None] * positions[None, None, :]


def mixed(form, first, second):
    return jnp.einsum(form, first, second, preferred_element_type=jnp.float32)


def receiver_fold(freqs, slow_rcv, locate, piece, start):
    part_real, part_imag = piece
    where = locate(start, part_real.shape[2])
    angle = phases(freqs, slow_rcv, where)
    steer_real = jnp.cos(angle).astype(jnp.bfloat16)
    steer_imag = jnp.sin(angle).astype(jnp.bfloat16)
    new_real = mixed("fab,fqb->faq", part_real, steer_real) - mixed(
        "fab,fqb->faq", part_imag, steer_imag
    )
    new_imag = mixed("fab,fqb->faq", part_real, steer_imag) + mixed(
        "fab,fqb->faq", part_imag, steer_real
    )
    return (new_real, new_imag)


def source_terms(freqs, slow_src, positions, focus_real, focus_imag):
    angle = phases(freqs, slow_src, positions)
    steer_real = jnp.cos(angle).astype(jnp.bfloat16)
    steer_imag = (-jnp.sin(angle)).astype(jnp.bfloat16)
    term_real = mixed("fpa,faq->pfq", steer_real, focus_real) - mixed(
        "fpa,faq->pfq", steer_imag, focus_imag
    )
    term_imag = mixed("fpa,faq->pfq", steer_real, focus_imag) + mixed(
        "fpa,faq->pfq", steer_imag, focus_real
    )
    return (term_real, term_imag)


def shards_any(src_real, src_imag, rcv_real, rcv_imag, src_pos, rcv_pos, freqs):
    n_time = lax.axis_size("tm")
    n_recv = lax.axis_size("rcv")
    n_source = lax.axis_size("src")
    src_block = src_real.shape[2]
    rcv_block = rcv_real.shape[2]
    windows = src_real.shape[1] * n_time
    q_block = RCV_SL // (n_time * n_recv)
    p_block = SRC_SL // n_source
    src_both = jnp.concatenate([src_real, src_imag], 1)
    rcv_plain = jnp.concatenate([rcv_real, rcv_imag], 1)
    rcv_turned = jnp.concatenate([-rcv_imag, rcv_real], 1)
    part_real = mixed("fwa,fwb->fab", src_both, rcv_plain)
    part_imag = mixed("fwa,fwb->fab", src_both, rcv_turned)
    q_first = (lax.axis_index("tm") * n_recv + lax.axis_index("rcv")) * q_block
    slow_rcv = grid_points(q_first, q_block, RCV_SL)
    sum_real, sum_imag = (
        lax.psum_scatter(part_real, "tm", scatter_dimension=2, tiled=True),
        lax.psum_scatter(part_imag, "tm", scatter_dimension=2, tiled=True),
    )
    sub_width = rcv_block // n_time

    def mapped(start, count):
        column = jnp.arange(count, dtype=jnp.int32)
        block = column // sub_width
        natural = block % n_recv * rcv_block + block // n_recv * sub_width + column % sub_width
        return jnp.take(rcv_pos, natural)

    cross = (sum_real.astype(jnp.bfloat16), sum_imag.astype(jnp.bfloat16))
    focus_real, focus_imag = receiver_fold(
        freqs,
        slow_rcv,
        mapped,
        (
            lax.all_gather(cross[0], ("tm", "rcv"), axis=2, tiled=True),
            lax.all_gather(cross[1], ("tm", "rcv"), axis=2, tiled=True),
        ),
        jnp.int32(0),
    )
    focus_scale = 1.0 / jnp.sqrt(jnp.float32(windows * RCV_ST))
    focus_real = (focus_real * focus_scale).astype(jnp.bfloat16)
    focus_imag = (focus_imag * focus_scale).astype(jnp.bfloat16)
    beam_scale = 1.0 / jnp.sqrt(jnp.float32(SRC_ST))
    own_pos = lax.dynamic_slice_in_dim(src_pos, lax.axis_index("src") * src_block, src_block)
    slow_src = grid_points(jnp.int32(0), p_block * lax.axis_size("src"), SRC_SL)
    term_real, term_imag = source_terms(freqs, slow_src, own_pos, focus_real, focus_imag)
    return lax.psum_scatter(
        jnp.stack([term_real, term_imag], 1) * beam_scale, "src", scatter_dimension=0, tiled=True
    )


FINE = 32
CHUNKS = 4
VMEM = 48 * 1024 * 1024


def waves(freq, slowness, positions):
    angle = ((TWO_PI * freq) * slowness)[:, None] * positions[None, :]
    return jnp.cos(angle), jnp.sin(angle)


def tables(freq, starts, total, positions):
    coarse = (2.0 * starts.astype(jnp.float32) + 1.0) / total - 1.0
    fine = 2.0 * jnp.arange(FINE, dtype=jnp.float32) / total
    return waves(freq, coarse, positions) + waves(freq, fine, positions)


def runs(first, count):
    return first + FINE * jnp.arange(count // FINE, dtype=jnp.int32)


def nt(first, second):
    return lax.dot_general(first, second, (((1,), (1,)), ((), ())), preferred_element_type=jnp.float32)


def steered_kernel(sign, scale, n_parts, cos_c, sin_c, cos_f, sin_f, *refs):
    parts, outs, (steer, spectra) = refs[:n_parts], refs[n_parts:-2], refs[-2:]
    step = pl.program_id(0)
    group = cos_c.shape[0]
    rows = group * FINE

    @pl.when(step == 0)
    def _():
        first = 0
        for part in parts:
            spectra[:, first : first + part.shape[1]] = part[...]
            first += part.shape[1]

    for i in range(group):
        cc, sc = cos_c[i : i + 1, :], sin_c[i : i + 1, :]
        steer[i * FINE : (i + 1) * FINE, :] = (cc * cos_f[...] - sc * sin_f[...]).astype(jnp.bfloat16)
        steer[rows + i * FINE : rows + (i + 1) * FINE, :] = (sc * cos_f[...] + cc * sin_f[...]).astype(
            jnp.bfloat16
        )
    found = nt(steer[...], spectra[...])
    half = found.shape[1] // 2
    real = (found[:rows, :half] + found[rows:, half:]) * scale
    imag = (found[:rows, half:] - found[rows:, :half]) * (sign * scale)
    for k, out in enumerate(outs):

        @pl.when(step == k)
        def _(out=out):
            if out.ndim == 2:
                out[:, :half] = real.astype(out.dtype)
                out[:, half:] = imag.astype(out.dtype)
            else:
                out[:, 0, :] = real
                out[:, 1, :] = imag


def steered(table, parts, steps, sign=1.0, scale=1.0, paired=False):
    coarse, depth = table[0].shape
    wide = parts[0].shape[0]
    group = coarse // steps
    rows = group * FINE
    whole = lambda v: pl.BlockSpec(v.shape, lambda i: (0, 0))
    if paired:
        shape, spec = jax.ShapeDtypeStruct((rows, 2, wide // 2), jnp.float32), pl.BlockSpec(
            (rows, 2, wide // 2), lambda i: (0, 0, 0)
        )
    else:
        shape, spec = jax.ShapeDtypeStruct((rows, wide), jnp.bfloat16), pl.BlockSpec((rows, wide), lambda i: (0, 0))
    return pl.pallas_call(
        lambda *refs: steered_kernel(sign, scale, len(parts), *refs),
        grid=(steps,),
        in_specs=[pl.BlockSpec((group, depth), lambda i: (i, 0))] * 2
        + [whole(v) for v in table[2:]]
        + [whole(v) for v in parts],
        out_specs=[spec] * steps,
        out_shape=[shape] * steps,
        scratch_shapes=[pltpu.VMEM((2 * rows, depth), jnp.bfloat16), pltpu.VMEM((wide, depth), jnp.bfloat16)],
        compiler_params=pltpu.CompilerParams(vmem_limit_bytes=VMEM),
        cost_estimate=pl.CostEstimate(
            flops=4 * coarse * FINE * wide * depth, bytes_accessed=2 * wide * depth, transcendentals=0
        ),
    )(*table, *parts)


def product_kernel(scale, own, near, mid, far, keep, send, here, over_y, over_x, over_xy, both):
    rows, wide = own.shape
    half = wide // 2
    first = 0
    for part in (own[...], near[...], mid[...] + far[...]):
        for at in range(0, part.shape[1], wide):
            real, imag = part[:, at : at + half], part[:, at + half : at + wide]
            both[:rows, first : first + half] = real
            both[:rows, first + half : first + wide] = -imag
            both[rows:, first : first + half] = imag
            both[rows:, first + half : first + wide] = real
            first += wide
    middle = rows // 2
    for side, one, two in ((keep, here, over_x), (send, over_y, over_xy)):
        total = nt(both[...], side[...]) * scale
        for t in range(2):
            one[:, t, :] = total[t * rows : t * rows + middle]
            two[:, t, :] = total[t * rows + middle : (t + 1) * rows]


def product(scale, own, near, mid, far, keep, send):
    rows = own.shape[0]
    shape = jax.ShapeDtypeStruct((rows // 2, 2, keep.shape[0]), jnp.float32)
    return pl.pallas_call(
        lambda *refs: product_kernel(scale, *refs),
        out_shape=[shape] * 4,
        in_specs=[pl.BlockSpec(memory_space=pltpu.VMEM)] * 6,
        out_specs=[pl.BlockSpec(memory_space=pltpu.VMEM)] * 4,
        scratch_shapes=[pltpu.VMEM((2 * rows, keep.shape[1]), jnp.bfloat16)],
        compiler_params=pltpu.CompilerParams(vmem_limit_bytes=VMEM),
        cost_estimate=pl.CostEstimate(
            flops=8 * rows * keep.shape[0] * keep.shape[1], bytes_accessed=4 * keep.size, transcendentals=0
        ),
    )(own, near, mid, far, keep, send)


def shards_plane(src_real, src_imag, rcv_real, rcv_imag, src_pos, rcv_pos, freqs):
    n_z = lax.axis_size("tm")
    bins, wide, a_block = src_real.shape
    b_block = rcv_real.shape[2]
    half = wide // 2
    p_block = SRC_SL // lax.axis_size("src")
    q_plane = RCV_SL // n_z
    q_block = q_plane // 2
    q_sub = q_block // lax.axis_size("src")
    z, s, y = (lax.axis_index(name) for name in ("tm", "src", "rcv"))
    x, c = s // 2, s % 2
    mine = 2 * x + y
    last = bins - 1
    inner = (z == 1) | (z == 2)
    core = lambda v: lax.ppermute(v, "src", [(i, i ^ 1) for i in range(4)])
    over_x = lambda v: lax.ppermute(v, "src", [(i, i ^ 2) for i in range(4)])
    over_y = lambda v: lax.ppermute(v, "rcv", [(0, 1), (1, 0)])
    over_xy = lambda v: lax.ppermute(v, ("src", "rcv"), [(i, i ^ 5) for i in range(8)])
    over_z = lambda v, d: lax.ppermute(v, "tm", [(i, i ^ d) for i in range(n_z)])

    def chain(v):
        near = over_z(v, 1)
        mid = lax.ppermute(jnp.concatenate([v, near], 1), "tm", [(1, 2), (2, 1)])
        far = lax.ppermute(mid, "tm", [(1, 0), (2, 3)])
        return v, near, mid, far

    def bin_of(real, imag, which):
        return jnp.stack([lax.dynamic_index_in_dim(part, which, 0, False) for part in (real, imag)])

    raw_last = lax.dynamic_slice_in_dim(jnp.stack([src_real[last], src_imag[last]]), y * half, half, 1)
    raw_last = chain(raw_last.reshape(2 * half, a_block))

    flat = lambda v: v.reshape(-1, v.shape[-1])
    given = over_x(flat(bin_of(src_real, src_imag, 2 * (1 - x) + y)))
    own = flat(bin_of(src_real, src_imag, mine))
    x_mine = [own, given, core(own), core(given)]
    theirs = jnp.stack([bin_of(rcv_real, rcv_imag, 2 * x + 1 - y), jnp.stack([rcv_real[last], rcv_imag[last]])])
    given = over_y(lax.dynamic_slice_in_dim(theirs, c * half, half, 2))
    other = core(given)
    given, other = jnp.where(c == 0, given, other), jnp.where(c == 0, other, given)
    given = jnp.concatenate([given, other], 2)
    y_mine = [flat(bin_of(rcv_real, rcv_imag, mine)), flat(given[0])]
    y_last = [flat(jnp.stack([rcv_real[last], rcv_imag[last]])), flat(given[1])]

    take = lambda v, block, size: lax.dynamic_slice_in_dim(v, block * size, size)
    at_src = jnp.concatenate([take(src_pos, block, a_block) for block in (s, s ^ 2, s ^ 1, s ^ 3)])
    at_rcv = jnp.concatenate([take(rcv_pos, block, b_block) for block in (y, 1 - y)])
    f_mine, f_last = lax.dynamic_index_in_dim(freqs, mine, 0, False), freqs[last]

    chunk = p_block // CHUNKS
    here, there = s * p_block, (s ^ 2) * p_block
    starts = jnp.concatenate(
        [runs(first + k * chunk, chunk) for k in range(CHUNKS) for first in (here, there)]
    )
    pieces = [chain(v) for v in steered(tables(f_mine, starts, SRC_SL, at_src), x_mine, CHUNKS)]

    planes = [z ^ d for d in range(n_z)]
    r_mine = tables(
        f_mine, jnp.concatenate([runs(to * q_plane + c * q_block, q_block) for to in planes]), RCV_SL, at_rcv
    )
    r_last = tables(
        f_last,
        jnp.concatenate([runs(to * q_plane + y * q_block + s * q_sub, q_sub) for to in planes]),
        RCV_SL,
        at_rcv,
    )
    yr_mine = steered(r_mine, y_mine, n_z, sign=-1.0)
    yr_last = steered(r_last, y_last, 1, sign=-1.0)[0].reshape(n_z, q_sub, -1)
    got = [jnp.concatenate([yr_mine[d], yr_last[d]], 0) for d in range(n_z)]
    got = [got[0]] + [over_z(got[d], d) for d in range(1, n_z)]
    got = [got[0], got[1], jnp.where(inner, got[3], got[2]), jnp.where(inner, got[2], got[3])]
    yr_mine = jnp.concatenate([v[:q_block] for v in got], 1)
    yr_last = jnp.concatenate([v[q_block:] for v in got], 1)

    yr_other = core(yr_mine)
    keep_mine = jnp.where(c == y, yr_mine, yr_other)
    send_mine = jnp.where(c == y, yr_other, yr_mine)
    yr_last = lax.all_gather(yr_last, "src", axis=0, tiled=True).reshape(q_block, n_z, 2, wide)

    focus_scale = 1.0 / float(wide * n_z * RCV_ST) ** 0.5
    beam_scale = 1.0 / float(SRC_ST) ** 0.5
    whole = jnp.zeros((p_block, bins, 2, q_block), jnp.float32)

    own, near, mid, far = raw_last
    slots = jnp.stack([own, near, (mid + far)[:, :a_block], (mid + far)[:, a_block:]])
    slots = slots.reshape(n_z, 2, half, a_block)
    other = over_y(slots)
    slots = jnp.concatenate([jnp.where(y == 0, slots, other), jnp.where(y == 0, other, slots)], 2)
    parts = jnp.einsum("qzuw,ztwa->utqa", yr_last, slots, preferred_element_type=jnp.float32) * focus_scale
    focus = jnp.concatenate([parts[0, 0] - parts[1, 1], parts[0, 1] + parts[1, 0]], 0).astype(jnp.bfloat16)
    table = tables(
        f_last,
        jnp.concatenate([runs(block * p_block, p_block) for block in (s, s ^ 2, s ^ 1, s ^ 3)]),
        SRC_SL,
        take(src_pos, s, a_block),
    )
    shares = steered(table, [focus], 4, scale=beam_scale, paired=True)
    shares = [shares[0] + core(shares[2]), shares[1] + core(shares[3])]
    shares = shares[0] + over_x(shares[1])
    whole = lax.dynamic_update_slice(whole, shares[:, None], (0, last, 0, 0))

    for k in range(CHUNKS):
        found = product(focus_scale * beam_scale, *pieces[k], keep_mine, send_mine)
        found = [found[0], over_y(found[1]), over_x(found[2]), over_xy(found[3])]
        for d in range(4):
            whole = lax.dynamic_update_slice(whole, found[d][:, None], (k * chunk, mine ^ d, 0, 0))
    return whole.transpose(0, 2, 1, 3)


def solution(mesh):
    plane = (mesh.shape["tm"], mesh.shape["src"], mesh.shape["rcv"]) == (4, 4, 2)
    shards = shards_plane if plane else shards_any
    in_specs = (
        P(None, "tm", "src"),
        P(None, "tm", "src"),
        P(None, "tm", "rcv"),
        P(None, "tm", "rcv"),
        P(),
        P(),
        P(),
    )
    out_specs = P("src", None, None, ("tm", "rcv"))
    return jax.shard_map(shards, mesh=mesh, in_specs=in_specs, out_specs=out_specs, check_vma=False)
```

```python
import jax
import jax.numpy as jnp
from jax import lax
from jax.experimental import pallas as pl
from jax.experimental.layout import Layout, with_layout_constraint
from jax.experimental.pallas import tpu as pltpu
from jax.sharding import PartitionSpec as P

SRC_ST = 2048
RCV_ST = 2048
SRC_SL = 2048
RCV_SL = 2048


TWO_PI = 6.283185307179586


def grid_points(first, count, total):
    index = (first + jnp.arange(count, dtype=jnp.int32)).astype(jnp.float32)
    return (2.0 * index + 1.0) / total - 1.0


def phases(freqs, slowness, positions):
    return (TWO_PI * freqs)[:, None, None] * slowness[None, :, None] * positions[None, None, :]


def mixed(form, first, second):
    return jnp.einsum(form, first, second, preferred_element_type=jnp.float32)


def receiver_fold(freqs, slow_rcv, locate, piece, start):
    part_real, part_imag = piece
    where = locate(start, part_real.shape[2])
    angle = phases(freqs, slow_rcv, where)
    steer_real = jnp.cos(angle).astype(jnp.bfloat16)
    steer_imag = jnp.sin(angle).astype(jnp.bfloat16)
    new_real = mixed("fab,fqb->faq", part_real, steer_real) - mixed(
        "fab,fqb->faq", part_imag, steer_imag
    )
    new_imag = mixed("fab,fqb->faq", part_real, steer_imag) + mixed(
        "fab,fqb->faq", part_imag, steer_real
    )
    return (new_real, new_imag)


def source_terms(freqs, slow_src, positions, focus_real, focus_imag):
    angle = phases(freqs, slow_src, positions)
    steer_real = jnp.cos(angle).astype(jnp.bfloat16)
    steer_imag = (-jnp.sin(angle)).astype(jnp.bfloat16)
    term_real = mixed("fpa,faq->pfq", steer_real, focus_real) - mixed(
        "fpa,faq->pfq", steer_imag, focus_imag
    )
    term_imag = mixed("fpa,faq->pfq", steer_real, focus_imag) + mixed(
        "fpa,faq->pfq", steer_imag, focus_real
    )
    return (term_real, term_imag)


def shards_any(src_real, src_imag, rcv_real, rcv_imag, src_pos, rcv_pos, freqs):
    n_time = lax.axis_size("tm")
    n_recv = lax.axis_size("rcv")
    n_source = lax.axis_size("src")
    src_block = src_real.shape[2]
    rcv_block = rcv_real.shape[2]
    windows = src_real.shape[1] * n_time
    q_block = RCV_SL // (n_time * n_recv)
    p_block = SRC_SL // n_source
    src_both = jnp.concatenate([src_real, src_imag], 1)
    rcv_plain = jnp.concatenate([rcv_real, rcv_imag], 1)
    rcv_turned = jnp.concatenate([-rcv_imag, rcv_real], 1)
    part_real = mixed("fwa,fwb->fab", src_both, rcv_plain)
    part_imag = mixed("fwa,fwb->fab", src_both, rcv_turned)
    q_first = (lax.axis_index("tm") * n_recv + lax.axis_index("rcv")) * q_block
    slow_rcv = grid_points(q_first, q_block, RCV_SL)
    sum_real, sum_imag = (
        lax.psum_scatter(part_real, "tm", scatter_dimension=2, tiled=True),
        lax.psum_scatter(part_imag, "tm", scatter_dimension=2, tiled=True),
    )
    sub_width = rcv_block // n_time

    def mapped(start, count):
        column = jnp.arange(count, dtype=jnp.int32)
        block = column // sub_width
        natural = block % n_recv * rcv_block + block // n_recv * sub_width + column % sub_width
        return jnp.take(rcv_pos, natural)

    cross = (sum_real.astype(jnp.bfloat16), sum_imag.astype(jnp.bfloat16))
    focus_real, focus_imag = receiver_fold(
        freqs,
        slow_rcv,
        mapped,
        (
            lax.all_gather(cross[0], ("tm", "rcv"), axis=2, tiled=True),
            lax.all_gather(cross[1], ("tm", "rcv"), axis=2, tiled=True),
        ),
        jnp.int32(0),
    )
    focus_scale = 1.0 / jnp.sqrt(jnp.float32(windows * RCV_ST))
    focus_real = (focus_real * focus_scale).astype(jnp.bfloat16)
    focus_imag = (focus_imag * focus_scale).astype(jnp.bfloat16)
    beam_scale = 1.0 / jnp.sqrt(jnp.float32(SRC_ST))
    own_pos = lax.dynamic_slice_in_dim(src_pos, lax.axis_index("src") * src_block, src_block)
    slow_src = grid_points(jnp.int32(0), p_block * lax.axis_size("src"), SRC_SL)
    term_real, term_imag = source_terms(freqs, slow_src, own_pos, focus_real, focus_imag)
    return lax.psum_scatter(
        jnp.stack([term_real, term_imag], 1) * beam_scale, "src", scatter_dimension=0, tiled=True
    )


FINE = 32
CHUNKS = 4
GROUPS = 2
ROWS = Layout(major_to_minor=(0, 1, 2, 3))
VMEM = 48 * 1024 * 1024


def waves(freq, slowness, positions):
    angle = ((TWO_PI * freq) * slowness)[:, None] * positions[None, :]
    return jnp.cos(angle), jnp.sin(angle)


def tables(freq, starts, total, positions):
    coarse = (2.0 * starts.astype(jnp.float32) + 1.0) / total - 1.0
    fine = 2.0 * jnp.arange(FINE, dtype=jnp.float32) / total
    return waves(freq, coarse, positions) + waves(freq, fine, positions)


def runs(first, count):
    return first + FINE * jnp.arange(count // FINE, dtype=jnp.int32)


def nt(first, second):
    return lax.dot_general(first, second, (((1,), (1,)), ((), ())), preferred_element_type=jnp.float32)


def steered_kernel(sign, scale, n_parts, cos_c, sin_c, cos_f, sin_f, *refs):
    parts, outs, (steer, spectra) = refs[:n_parts], refs[n_parts:-2], refs[-2:]
    step = pl.program_id(0)
    group = cos_c.shape[0]
    rows = group * FINE

    @pl.when(step == 0)
    def _():
        first = 0
        for part in parts:
            spectra[:, first : first + part.shape[1]] = part[...]
            first += part.shape[1]

    for i in range(group):
        cc, sc = cos_c[i : i + 1, :], sin_c[i : i + 1, :]
        steer[i * FINE : (i + 1) * FINE, :] = (cc * cos_f[...] - sc * sin_f[...]).astype(jnp.bfloat16)
        steer[rows + i * FINE : rows + (i + 1) * FINE, :] = (sc * cos_f[...] + cc * sin_f[...]).astype(
            jnp.bfloat16
        )
    found = nt(steer[...], spectra[...])
    half = found.shape[1] // 2
    real = (found[:rows, :half] + found[rows:, half:]) * scale
    imag = (found[:rows, half:] - found[rows:, :half]) * (sign * scale)
    for k, out in enumerate(outs):

        @pl.when(step == k)
        def _(out=out):
            if out.ndim == 2:
                out[:, :half] = real.astype(out.dtype)
                out[:, half:] = imag.astype(out.dtype)
            else:
                out[:, 0, :] = real
                out[:, 1, :] = imag


def steered(table, parts, steps, sign=1.0, scale=1.0, paired=False):
    coarse, depth = table[0].shape
    wide = parts[0].shape[0]
    group = coarse // steps
    rows = group * FINE
    whole = lambda v: pl.BlockSpec(v.shape, lambda i: (0, 0))
    if paired:
        shape, spec = jax.ShapeDtypeStruct((rows, 2, wide // 2), jnp.float32), pl.BlockSpec(
            (rows, 2, wide // 2), lambda i: (0, 0, 0)
        )
    else:
        shape, spec = jax.ShapeDtypeStruct((rows, wide), jnp.bfloat16), pl.BlockSpec((rows, wide), lambda i: (0, 0))
    return pl.pallas_call(
        lambda *refs: steered_kernel(sign, scale, len(parts), *refs),
        grid=(steps,),
        in_specs=[pl.BlockSpec((group, depth), lambda i: (i, 0))] * 2
        + [whole(v) for v in table[2:]]
        + [whole(v) for v in parts],
        out_specs=[spec] * steps,
        out_shape=[shape] * steps,
        scratch_shapes=[pltpu.VMEM((2 * rows, depth), jnp.bfloat16), pltpu.VMEM((wide, depth), jnp.bfloat16)],
        compiler_params=pltpu.CompilerParams(vmem_limit_bytes=VMEM),
        cost_estimate=pl.CostEstimate(
            flops=4 * coarse * FINE * wide * depth, bytes_accessed=2 * wide * depth, transcendentals=0
        ),
    )(*table, *parts)


def product_kernel(scale, first, own, near, one, two, three, four, keep, send, *refs):
    outs, both = refs[:-1], refs[-1]
    rows = both.shape[0] // 2
    wide = own.shape[1]
    half = wide // 2
    here = pl.ds(first, rows)
    for slot, part in enumerate((own[here, :], near[here, :], one[here, :] + two[here, :], three[here, :] + four[...])):
        at = slot * wide
        real, imag = part[:, :half], part[:, half:]
        both[:rows, at : at + half] = real
        both[:rows, at + half : at + wide] = -imag
        both[rows:, at : at + half] = imag
        both[rows:, at + half : at + wide] = real
    middle = rows // 2
    for side, one, two in ((keep, outs[0], outs[2]), (send, outs[1], outs[3])):
        total = nt(both[...], side[...]) * scale
        for t in range(2):
            one[:, t, :] = total[t * rows : t * rows + middle].astype(one.dtype)
            two[:, t, :] = total[t * rows + middle : (t + 1) * rows].astype(two.dtype)


def product(scale, first, rows, parts, keep, send):
    shape = (rows // 2, 2, keep.shape[0])
    return pl.pallas_call(
        lambda *refs: product_kernel(scale, first, *refs),
        out_shape=[jax.ShapeDtypeStruct(shape, kind) for kind in (jnp.float32,) + (jnp.bfloat16,) * 3],
        in_specs=[pl.BlockSpec(memory_space=pltpu.VMEM)] * 8,
        out_specs=[pl.BlockSpec(memory_space=pltpu.VMEM)] * 4,
        scratch_shapes=[pltpu.VMEM((2 * rows, keep.shape[1]), jnp.bfloat16)],
        compiler_params=pltpu.CompilerParams(vmem_limit_bytes=VMEM),
        cost_estimate=pl.CostEstimate(
            flops=8 * rows * keep.shape[0] * keep.shape[1], bytes_accessed=4 * keep.size, transcendentals=0
        ),
    )(*parts, keep, send)


def shards_plane(src_real, src_imag, rcv_real, rcv_imag, src_pos, rcv_pos, freqs):
    n_z = lax.axis_size("tm")
    bins, wide, a_block = src_real.shape
    b_block = rcv_real.shape[2]
    half = wide // 2
    p_block = SRC_SL // lax.axis_size("src")
    q_plane = RCV_SL // n_z
    q_block = q_plane // 2
    q_sub = q_block // lax.axis_size("src")
    z, s, y = (lax.axis_index(name) for name in ("tm", "src", "rcv"))
    x, c = s // 2, s % 2
    mine = 2 * x + y
    last = bins - 1
    inner = (z == 1) | (z == 2)
    core = lambda v: lax.ppermute(v, "src", [(i, i ^ 1) for i in range(4)])
    over_x = lambda v: lax.ppermute(v, "src", [(i, i ^ 2) for i in range(4)])
    over_y = lambda v: lax.ppermute(v, "rcv", [(0, 1), (1, 0)])
    over_xy = lambda v: lax.ppermute(v, ("src", "rcv"), [(i, i ^ 5) for i in range(8)])
    over_z = lambda v, d: lax.ppermute(v, "tm", [(i, i ^ d) for i in range(n_z)])

    turn = [freqs]

    def after(v, *others):
        return lax.optimization_barrier((v, others))[0]

    def step(v):
        v = after(v, turn[0])
        turn[0] = v
        return v

    ends = lambda v: lax.ppermute(v, "tm", [(1, 0), (2, 3)])
    middle = lambda v: lax.ppermute(v, "tm", [(1, 2), (2, 1)])

    def bin_of(real, imag, which):
        return jnp.stack([lax.dynamic_index_in_dim(part, which, 0, False) for part in (real, imag)])

    flat = lambda v: v.reshape(-1, v.shape[-1])
    given = step(flat(bin_of(src_real, src_imag, 2 * (1 - x) + y)))
    given = over_x(given)
    raw_last = lax.dynamic_slice_in_dim(jnp.stack([src_real[last], src_imag[last]]), y * half, half, 1)
    raw_last = step(raw_last.reshape(2 * half, a_block))
    raw_near = over_z(raw_last, 1)
    raw_one = middle(raw_last)

    def half_bin(which):
        at = (which, c * half, 0)
        return jnp.concatenate([lax.dynamic_slice(v, at, (1, half, b_block))[0] for v in (rcv_real, rcv_imag)], 0)

    y_given = [half_bin(2 * x + 1 - y), half_bin(last)]
    y_given = [over_y(step(v)) for v in y_given]
    own = step(flat(bin_of(src_real, src_imag, mine)))
    x_mine = [own, given, core(own)]
    raw_near = step(raw_near)
    raw_two = middle(raw_near)
    raw_three = ends(step(raw_one))
    x_mine[1] = step(x_mine[1])
    x_mine.append(core(x_mine[1]))
    raw_two = step(raw_two)
    raw_four = ends(raw_two)
    take = lambda v, block, size: lax.dynamic_slice_in_dim(v, block * size, size)
    at_src = jnp.concatenate([take(src_pos, block, a_block) for block in (s, s ^ 2, s ^ 1, s ^ 3)])
    at_rcv = jnp.concatenate([take(rcv_pos, block, b_block) for block in (y, 1 - y)])
    f_mine, f_last = lax.dynamic_index_in_dim(freqs, mine, 0, False), freqs[last]

    chunk = p_block // CHUNKS
    here, there = s * p_block, (s ^ 2) * p_block
    starts = jnp.concatenate(
        [runs(first + k * chunk, chunk) for k in range(CHUNKS) for first in (here, there)]
    )
    pieces = steered(tables(f_mine, starts, SRC_SL, at_src), x_mine, GROUPS)
    pieces = step(pieces)
    near = [over_z(v, 1) for v in pieces]
    one = [middle(v) for v in pieces]
    raw_three, raw_four = step((raw_three, raw_four))
    slots = jnp.stack([raw_last, raw_near, raw_one + raw_three, raw_two + raw_four])
    slots = step(slots.reshape(n_z, 2, half, a_block))
    other_slots = over_y(slots)
    rcv_real, rcv_imag = after((rcv_real, rcv_imag), pieces[0])

    def receivers(which, given):
        given = step(given)
        other = core(given)
        pair = jnp.stack([jnp.where(c == 0, given, other), jnp.where(c == 0, other, given)])
        pair = pair.reshape(2, 2, half, b_block).transpose(1, 0, 2, 3).reshape(2 * wide, b_block)
        return [flat(bin_of(rcv_real, rcv_imag, which)), pair]

    y_mine, y_last = receivers(mine, y_given[0]), receivers(last, y_given[1])

    planes = [z ^ d for d in range(n_z)]
    r_mine = tables(
        f_mine, jnp.concatenate([runs(to * q_plane + c * q_block, q_block) for to in planes]), RCV_SL, at_rcv
    )
    r_last = tables(
        f_last,
        jnp.concatenate([runs(to * q_plane + y * q_block + s * q_sub, q_sub) for to in planes]),
        RCV_SL,
        at_rcv,
    )
    yr_mine = steered(r_mine, y_mine, n_z, sign=-1.0)
    yr_last = steered(r_last, y_last, 1, sign=-1.0)[0].reshape(n_z, q_sub, -1)
    got = step([jnp.concatenate([yr_mine[d], yr_last[d]], 0) for d in range(n_z)])
    got = [got[0]] + [over_z(got[d], d) for d in range(1, n_z)]
    two, three, four = [], [], []
    for k in range(GROUPS):
        near[k] = step(near[k])
        two.append(middle(near[k]))
        one[k] = step(one[k])
        three.append(ends(one[k]))
    got = step(got)
    got = [got[0], got[1], jnp.where(inner, got[3], got[2]), jnp.where(inner, got[2], got[3])]
    yr_mine = jnp.concatenate([v[:q_block] for v in got], 1)
    yr_last = jnp.concatenate([v[q_block:] for v in got], 1)
    yr_mine = step(yr_mine)
    yr_other = core(yr_mine)
    keep_mine = jnp.where(c == y, yr_mine, yr_other)
    send_mine = jnp.where(c == y, yr_other, yr_mine)
    three = step(three)
    yr_last = lax.all_gather(yr_last, "src", axis=0, tiled=True).reshape(q_block, n_z, 2, wide)
    per = CHUNKS // GROUPS
    for k in range(GROUPS):
        two[k] = step(two[k])
        four.append([ends(two[k][i * 2 * chunk : (i + 1) * 2 * chunk]) for i in range(per)])

    focus_scale = 1.0 / float(wide * n_z * RCV_ST) ** 0.5
    beam_scale = 1.0 / float(SRC_ST) ** 0.5
    whole = with_layout_constraint(jnp.zeros((p_block, bins, 2, q_block), jnp.float32), ROWS)

    other_slots = step(other_slots)
    slots = jnp.concatenate([jnp.where(y == 0, slots, other_slots), jnp.where(y == 0, other_slots, slots)], 2)
    parts = jnp.einsum("qzuw,ztwa->utqa", yr_last, slots, preferred_element_type=jnp.float32) * focus_scale
    focus = jnp.concatenate([parts[0, 0] - parts[1, 1], parts[0, 1] + parts[1, 0]], 0).astype(jnp.bfloat16)
    table = tables(
        f_last,
        jnp.concatenate([runs(block * p_block, p_block) for block in (s, s ^ 2, s ^ 1, s ^ 3)]),
        SRC_SL,
        take(src_pos, s, a_block),
    )
    shares = steered(table, [focus], 4, scale=beam_scale, paired=True)
    shares = [shares[0] + core(shares[2]), shares[1] + core(shares[3])]
    shares = shares[0] + over_x(shares[1])
    whole = lax.dynamic_update_slice(whole, shares[:, None], (0, last, 0, 0))

    for k in range(CHUNKS):
        g, i = k // per, k % per
        parts = [pieces[g], near[g], one[g], three[g], two[g], step(four[g][i])]
        found = product(focus_scale * beam_scale, i * 2 * chunk, 2 * chunk, parts, keep_mine, send_mine)
        found = step(found)
        found = [found[0], over_y(found[1]), over_x(found[2]), over_xy(found[3])]
        for d in range(4):
            whole = lax.dynamic_update_slice(whole, found[d].astype(jnp.float32)[:, None], (k * chunk, mine ^ d, 0, 0))
    return with_layout_constraint(whole, ROWS).transpose(0, 2, 1, 3)


def solution(mesh):
    plane = (mesh.shape["tm"], mesh.shape["src"], mesh.shape["rcv"]) == (4, 4, 2)
    shards = shards_plane if plane else shards_any
    in_specs = (
        P(None, "tm", "src"),
        P(None, "tm", "src"),
        P(None, "tm", "rcv"),
        P(None, "tm", "rcv"),
        P(),
        P(),
        P(),
    )
    out_specs = P("src", None, None, ("tm", "rcv"))
    return jax.shard_map(shards, mesh=mesh, in_specs=in_specs, out_specs=out_specs, check_vma=False)
```

```python
import jax
import jax.numpy as jnp
from jax import lax
from jax.experimental import pallas as pl
from jax.experimental.pallas import tpu as pltpu
from jax.sharding import PartitionSpec as P

SRC_ST = 2048
RCV_ST = 2048
SRC_SL = 2048
RCV_SL = 2048


TWO_PI = 6.283185307179586


def grid_points(first, count, total):
    index = (first + jnp.arange(count, dtype=jnp.int32)).astype(jnp.float32)
    return (2.0 * index + 1.0) / total - 1.0


def phases(freqs, slowness, positions):
    return (TWO_PI * freqs)[:, None, None] * slowness[None, :, None] * positions[None, None, :]


def mixed(form, first, second):
    return jnp.einsum(form, first, second, preferred_element_type=jnp.float32)


def receiver_fold(freqs, slow_rcv, locate, piece, start):
    part_real, part_imag = piece
    where = locate(start, part_real.shape[2])
    angle = phases(freqs, slow_rcv, where)
    steer_real = jnp.cos(angle).astype(jnp.bfloat16)
    steer_imag = jnp.sin(angle).astype(jnp.bfloat16)
    new_real = mixed("fab,fqb->faq", part_real, steer_real) - mixed(
        "fab,fqb->faq", part_imag, steer_imag
    )
    new_imag = mixed("fab,fqb->faq", part_real, steer_imag) + mixed(
        "fab,fqb->faq", part_imag, steer_real
    )
    return (new_real, new_imag)


def source_terms(freqs, slow_src, positions, focus_real, focus_imag):
    angle = phases(freqs, slow_src, positions)
    steer_real = jnp.cos(angle).astype(jnp.bfloat16)
    steer_imag = (-jnp.sin(angle)).astype(jnp.bfloat16)
    term_real = mixed("fpa,faq->pfq", steer_real, focus_real) - mixed(
        "fpa,faq->pfq", steer_imag, focus_imag
    )
    term_imag = mixed("fpa,faq->pfq", steer_real, focus_imag) + mixed(
        "fpa,faq->pfq", steer_imag, focus_real
    )
    return (term_real, term_imag)


def shards_any(src_real, src_imag, rcv_real, rcv_imag, src_pos, rcv_pos, freqs):
    n_time = lax.axis_size("tm")
    n_recv = lax.axis_size("rcv")
    n_source = lax.axis_size("src")
    src_block = src_real.shape[2]
    rcv_block = rcv_real.shape[2]
    windows = src_real.shape[1] * n_time
    q_block = RCV_SL // (n_time * n_recv)
    p_block = SRC_SL // n_source
    src_both = jnp.concatenate([src_real, src_imag], 1)
    rcv_plain = jnp.concatenate([rcv_real, rcv_imag], 1)
    rcv_turned = jnp.concatenate([-rcv_imag, rcv_real], 1)
    part_real = mixed("fwa,fwb->fab", src_both, rcv_plain)
    part_imag = mixed("fwa,fwb->fab", src_both, rcv_turned)
    q_first = (lax.axis_index("tm") * n_recv + lax.axis_index("rcv")) * q_block
    slow_rcv = grid_points(q_first, q_block, RCV_SL)
    sum_real, sum_imag = (
        lax.psum_scatter(part_real, "tm", scatter_dimension=2, tiled=True),
        lax.psum_scatter(part_imag, "tm", scatter_dimension=2, tiled=True),
    )
    sub_width = rcv_block // n_time

    def mapped(start, count):
        column = jnp.arange(count, dtype=jnp.int32)
        block = column // sub_width
        natural = block % n_recv * rcv_block + block // n_recv * sub_width + column % sub_width
        return jnp.take(rcv_pos, natural)

    cross = (sum_real.astype(jnp.bfloat16), sum_imag.astype(jnp.bfloat16))
    focus_real, focus_imag = receiver_fold(
        freqs,
        slow_rcv,
        mapped,
        (
            lax.all_gather(cross[0], ("tm", "rcv"), axis=2, tiled=True),
            lax.all_gather(cross[1], ("tm", "rcv"), axis=2, tiled=True),
        ),
        jnp.int32(0),
    )
    focus_scale = 1.0 / jnp.sqrt(jnp.float32(windows * RCV_ST))
    focus_real = (focus_real * focus_scale).astype(jnp.bfloat16)
    focus_imag = (focus_imag * focus_scale).astype(jnp.bfloat16)
    beam_scale = 1.0 / jnp.sqrt(jnp.float32(SRC_ST))
    own_pos = lax.dynamic_slice_in_dim(src_pos, lax.axis_index("src") * src_block, src_block)
    slow_src = grid_points(jnp.int32(0), p_block * lax.axis_size("src"), SRC_SL)
    term_real, term_imag = source_terms(freqs, slow_src, own_pos, focus_real, focus_imag)
    return lax.psum_scatter(
        jnp.stack([term_real, term_imag], 1) * beam_scale, "src", scatter_dimension=0, tiled=True
    )


FINE = 32
CHUNKS = 2
PLACE_Y, CORE, INNER, SAME, MINE, PLACE_X = range(6)
VMEM = 48 * 1024 * 1024


def waves(freq, slowness, positions):
    angle = ((TWO_PI * freq) * slowness)[:, None] * positions[None, :]
    return jnp.cos(angle), jnp.sin(angle)


def tables(freq, starts, total, positions):
    coarse = (2.0 * starts.astype(jnp.float32) + 1.0) / total - 1.0
    fine = 2.0 * jnp.arange(FINE, dtype=jnp.float32) / total
    return waves(freq, coarse, positions) + waves(freq, fine, positions)


def nt(first, second):
    return lax.dot_general(first, second, (((1,), (1,)), ((), ())), preferred_element_type=jnp.float32)


def steered_kernel(sign, scale, n_parts, n_halves, flags, cos_c, sin_c, cos_f, sin_f, *refs):
    parts, halves = refs[:n_parts], refs[n_parts : n_parts + n_halves]
    outs, (steer, spectra) = refs[n_parts + n_halves : -2], refs[-2:]
    step = pl.program_id(0)
    group = cos_c.shape[0]
    rows = group * FINE

    @pl.when(step == 0)
    def _():
        first = 0
        for part in parts:
            spectra[:, first : first + part.shape[1]] = part[...]
            first += part.shape[1]
        for i, part in enumerate(halves):
            count = part.shape[0] // 2
            for t in range(2):
                at = 2 * t * count + (flags[CORE] if i == 0 else 1 - flags[CORE]) * count
                spectra[pl.ds(pl.multiple_of(at, count), count), first:] = part[t * count : (t + 1) * count, :]

    for i in range(group):
        cc, sc = cos_c[i : i + 1, :], sin_c[i : i + 1, :]
        steer[i * FINE : (i + 1) * FINE, :] = (cc * cos_f[...] - sc * sin_f[...]).astype(jnp.bfloat16)
        steer[rows + i * FINE : rows + (i + 1) * FINE, :] = (sc * cos_f[...] + cc * sin_f[...]).astype(
            jnp.bfloat16
        )
    found = nt(steer[...], spectra[...])
    half = found.shape[1] // 2
    real = (found[:rows, :half] + found[rows:, half:]) * scale
    imag = (found[:rows, half:] - found[rows:, :half]) * (sign * scale)
    for k, out in enumerate(outs):

        size = out.shape[0]
        per = rows // size

        @pl.when((step == k // per) | (len(outs) == 1))
        def _(out=out, at=k % per * size):
            if out.ndim == 2:
                out[:, :half] = real[at : at + size].astype(out.dtype)
                out[:, half:] = imag[at : at + size].astype(out.dtype)
            else:
                out[:, 0, :] = real.astype(out.dtype)
                out[:, 1, :] = imag.astype(out.dtype)


def steered(flags, table, parts, steps, halves=(), cuts=1, sign=1.0, scale=1.0, paired=False, joined=False):
    coarse, depth = table[0].shape
    wide = parts[0].shape[0]
    group = coarse // steps
    rows = group * FINE
    whole = lambda v: pl.BlockSpec(v.shape, lambda i: (0, 0))
    if paired:
        shape, spec = jax.ShapeDtypeStruct((rows, 2, wide // 2), jnp.float32), pl.BlockSpec(
            (rows, 2, wide // 2), lambda i: (0, 0, 0)
        )
    else:
        shape, spec = jax.ShapeDtypeStruct((rows, wide), jnp.bfloat16), pl.BlockSpec((rows, wide), lambda i: (0, 0))
    shapes, specs = [shape] * steps, [spec] * steps
    if paired:
        shapes[1:] = [jax.ShapeDtypeStruct(shape.shape, jnp.bfloat16)] * (steps - 1)
    if cuts > 1:
        shapes = [jax.ShapeDtypeStruct((rows // cuts, wide), jnp.bfloat16)] * (steps * cuts)
        specs = [pl.BlockSpec((rows // cuts, wide), lambda i: (0, 0))] * (steps * cuts)
    if joined:
        shapes = jax.ShapeDtypeStruct((steps * rows, wide), jnp.bfloat16)
        specs = pl.BlockSpec((rows, wide), lambda i: (i, 0))
    return pl.pallas_call(
        lambda *refs: steered_kernel(sign, scale, len(parts), len(halves), *refs),
        grid=(steps,),
        in_specs=[pl.BlockSpec(memory_space=pltpu.SMEM)]
        + [pl.BlockSpec((group, depth), lambda i: (i, 0))] * 2
        + [whole(v) for v in (*table[2:], *parts, *halves)],
        out_specs=specs,
        out_shape=shapes,
        scratch_shapes=[pltpu.VMEM((2 * rows, depth), jnp.bfloat16), pltpu.VMEM((wide, depth), jnp.bfloat16)],
        compiler_params=pltpu.CompilerParams(vmem_limit_bytes=VMEM),
        cost_estimate=pl.CostEstimate(flops=1, bytes_accessed=1, transcendentals=0),
    )(flags, *table, *parts, *halves)


def focus_kernel(scale, flags, slots, others, receiver, out, real, imag, both):
    n_z, rows, _ = slots.shape
    half = rows // 2
    wide = rows
    part = receiver.shape[1]
    q = 2 * part
    for slot in range(n_z):
        for v, at in ((slots, flags[PLACE_Y] * half), (others, (1 - flags[PLACE_Y]) * half)):
            to = pl.ds(pl.multiple_of(slot * wide + at, half), half)
            real[to, :] = v[slot, :half, :]
            imag[to, :] = v[slot, half:, :]
        for t in range(2):
            for i in range(receiver.shape[0]):
                row, col = t * q + i % 2 * part, slot * wide + i // 2 * half
                both[row : row + part, col : col + half] = receiver[i, :, (2 * slot + t) * half : (2 * slot + t + 1) * half]
    one = jnp.dot(both[...], real[...], preferred_element_type=jnp.float32)
    two = jnp.dot(both[...], imag[...], preferred_element_type=jnp.float32)
    out[:q, :] = ((one[:q] - two[q:]) * scale).astype(out.dtype)
    out[q:, :] = ((one[q:] + two[:q]) * scale).astype(out.dtype)


def focused(scale, flags, slots, others, receiver):
    n_z, rows, stations = slots.shape
    q = 2 * receiver.shape[1]
    vmem = pl.BlockSpec(memory_space=pltpu.VMEM)
    return pl.pallas_call(
        lambda *refs: focus_kernel(scale, *refs),
        out_shape=jax.ShapeDtypeStruct((2 * q, stations), jnp.bfloat16),
        in_specs=[pl.BlockSpec(memory_space=pltpu.SMEM)] + [vmem] * 3,
        out_specs=vmem,
        scratch_shapes=[pltpu.VMEM((n_z * rows, stations), jnp.bfloat16)] * 2
        + [pltpu.VMEM((2 * q, n_z * rows), jnp.bfloat16)],
        compiler_params=pltpu.CompilerParams(vmem_limit_bytes=VMEM),
        cost_estimate=pl.CostEstimate(flops=1, bytes_accessed=1, transcendentals=0),
    )(flags, slots, others, receiver)


def product_kernel(scale, flags, own, near, one, two, three, four, mine, other, *refs):
    outs, both = refs[:-1], refs[-1]
    rows = both.shape[0] // 2
    wide = own.shape[1]
    half = wide // 2
    for slot, part in enumerate((own[...], near[...], one[...] + two[...], three[...] + four[...])):
        at = slot * wide
        real, imag = part[:, :half], part[:, half:]
        both[:rows, at : at + half] = real
        both[:rows, at + half : at + wide] = -imag
        both[rows:, at : at + half] = imag
        both[rows:, at + half : at + wide] = real
    middle = rows // 2
    same = flags[SAME] == 1
    by_mine, by_other = nt(both[...], mine[...]) * scale, nt(both[...], other[...]) * scale
    for total, one, two in (
        (jnp.where(same, by_mine, by_other), outs[0], outs[2]),
        (jnp.where(same, by_other, by_mine), outs[1], outs[3]),
    ):
        for t in range(2):
            one[:, t, :] = total[t * rows : t * rows + middle].astype(one.dtype)
            two[:, t, :] = total[t * rows + middle : (t + 1) * rows].astype(two.dtype)


def product(scale, k, rows, flags, parts, mine, other):
    shape = (rows // 2, 2, mine.shape[0])
    return pl.pallas_call(
        lambda *refs: product_kernel(scale, *refs),
        grid=(1,),
        out_shape=[jax.ShapeDtypeStruct(shape, kind) for kind in (jnp.float32,) + (jnp.bfloat16,) * 3],
        in_specs=[pl.BlockSpec(memory_space=pltpu.SMEM)]
        + [pl.BlockSpec((rows, v.shape[1]), lambda i: (k, 0)) for v in parts[:-1]]
        + [pl.BlockSpec(v.shape, lambda i: (0, 0)) for v in (parts[-1], mine, other)],
        out_specs=[pl.BlockSpec(shape, lambda i: (0, 0, 0))] * 4,
        scratch_shapes=[pltpu.VMEM((2 * rows, mine.shape[1]), jnp.bfloat16)],
        compiler_params=pltpu.CompilerParams(vmem_limit_bytes=VMEM),
        cost_estimate=pl.CostEstimate(flops=1, bytes_accessed=1, transcendentals=0),
    )(flags, *parts, mine, other)


def arranged_kernel(flags, own, one, two, three, out):
    inner = flags[INNER] == 1
    second, third = jnp.where(inner, three[...], two[...]), jnp.where(inner, two[...], three[...])
    wide = own.shape[1]
    for slot, v in enumerate((own[...], one[...], second, third)):
        if out.ndim == 3:
            out[slot] = v
        else:
            out[:, slot * wide : (slot + 1) * wide] = v


def arranged(flags, got, stacked):
    rows, wide = got[0].shape
    vmem = pl.BlockSpec(memory_space=pltpu.VMEM)
    return pl.pallas_call(
        arranged_kernel,
        out_shape=jax.ShapeDtypeStruct((4, rows, wide) if stacked else (rows, 4 * wide), got[0].dtype),
        in_specs=[pl.BlockSpec(memory_space=pltpu.SMEM)] + [vmem] * 4,
        out_specs=vmem,
        compiler_params=pltpu.CompilerParams(vmem_limit_bytes=VMEM),
        cost_estimate=pl.CostEstimate(flops=1, bytes_accessed=1, transcendentals=0),
    )(flags, *got)


def fill_steering(steer, cos_c, sin_c, cos_f, sin_f, first, count):
    for i in range(count):
        cc, sc = cos_c[pl.ds(first + i, 1), :], sin_c[pl.ds(first + i, 1), :]
        steer[i * FINE : (i + 1) * FINE, :] = (cc * cos_f[...] - sc * sin_f[...]).astype(steer.dtype)
        steer[(count + i) * FINE : (count + i + 1) * FINE, :] = (sc * cos_f[...] + cc * sin_f[...]).astype(
            steer.dtype
        )


def conjugated(steer, spectra):
    found = nt(steer[...], spectra[...])
    rows, half = found.shape[0] // 2, found.shape[1] // 2
    return found[:rows, :half] + found[rows:, half:], found[rows:, :half] - found[:rows, half:]


def receivers_kernel(flags, *refs):
    tables, own, own_last, (given, other) = (refs[:4], refs[4:8]), refs[8:10], refs[10:12], refs[12:14]
    outs, (steer, spectra, steer_last, spectra_last) = refs[14:-4], refs[-4:]
    step = pl.program_id(0)

    @pl.when(step == 0)
    def _():
        first = 0
        for to, here in ((spectra, own), (spectra_last, own_last)):
            b_block, count = here[0].shape[2], here[0].shape[1] // 2
            to[: 2 * count, :b_block] = here[0][0]
            to[2 * count :, :b_block] = here[1][0]
            for t in range(2):
                rows = slice(first + t * count, first + (t + 1) * count)
                for part, place in ((given, flags[CORE]), (other, 1 - flags[CORE])):
                    at = pl.multiple_of((2 * t + place) * count, count)
                    to[pl.ds(at, count), b_block:] = part[rows, :]
            first += 2 * count

    coarse = tables[0][0].shape[0]
    fill_steering(steer, *tables[0], 0, coarse)
    real, imag = conjugated(steer, spectra)
    coarse_last = tables[1][0].shape[0] // len(outs)
    fill_steering(steer_last, *tables[1], step * coarse_last, coarse_last)
    real_last, imag_last = conjugated(steer_last, spectra_last)
    rows, wide = real.shape
    half, part = real_last.shape[0] // 2, wide // 2
    for k, out in enumerate(outs):

        @pl.when(step == k)
        def _(out=out):
            out[:rows, :wide] = real.astype(out.dtype)
            out[:rows, wide:] = imag.astype(out.dtype)
            for i in range(2):
                at = slice(i * half, (i + 1) * half)
                out[rows:, 2 * i * part : (2 * i + 1) * part] = real_last[at].astype(out.dtype)
                out[rows:, (2 * i + 1) * part : (2 * i + 2) * part] = imag_last[at].astype(out.dtype)


def receivers_of(flags, table, table_last, real, imag, given, other):
    planes = 4
    bins, wide, b_block = real.shape
    coarse, depth = table[0].shape
    rows, rows_last = coarse * FINE // planes, table_last[0].shape[0] * FINE // planes
    shape = jax.ShapeDtypeStruct((rows + rows_last // 2, 2 * wide), jnp.bfloat16)
    whole = lambda v: pl.BlockSpec(v.shape, lambda i, f: (0, 0))
    return pl.pallas_call(
        receivers_kernel,
        grid_spec=pltpu.PrefetchScalarGridSpec(
            num_scalar_prefetch=1,
            grid=(planes,),
            in_specs=[pl.BlockSpec((coarse // planes, depth), lambda i, f: (i, 0))] * 2
            + [whole(v) for v in (*table[2:], *table_last)]
            + [pl.BlockSpec((1, wide, b_block), lambda i, f: (f[MINE], 0, 0))] * 2
            + [pl.BlockSpec((1, wide // 2, b_block), lambda i, f: (bins - 1, f[PLACE_X], 0))] * 2
            + [whole(given), whole(other)],
            out_specs=[pl.BlockSpec(shape.shape, lambda i, f: (0, 0))] * planes,
            scratch_shapes=[
                pltpu.VMEM((2 * rows, depth), jnp.bfloat16),
                pltpu.VMEM((2 * wide, depth), jnp.bfloat16),
                pltpu.VMEM((2 * rows_last, depth), jnp.bfloat16),
                pltpu.VMEM((wide, depth), jnp.bfloat16),
            ],
        ),
        out_shape=[shape] * planes,
        compiler_params=pltpu.CompilerParams(vmem_limit_bytes=VMEM),
        cost_estimate=pl.CostEstimate(flops=1, bytes_accessed=1, transcendentals=0),
    )(flags, *table, *table_last, real, imag, real, imag, given, other)


def parted_kernel(flags, own, one, two, three, out, out_last):
    inner = flags[INNER] == 1
    second, third = jnp.where(inner, three[...], two[...]), jnp.where(inner, two[...], three[...])
    wide, half, rows = own.shape[1], own.shape[1] // 2, out.shape[0]
    rest = own.shape[0] - rows
    for slot, v in enumerate((own[...], one[...], second, third)):
        out[:, slot * wide : (slot + 1) * wide] = v[:rows]
        for i in range(2):
            out_last[i * rest : (i + 1) * rest, slot * half : (slot + 1) * half] = v[rows:, i * half : (i + 1) * half]


def parted(flags, got, rows):
    vmem = pl.BlockSpec(memory_space=pltpu.VMEM)
    high, wide = got[0].shape
    return pl.pallas_call(
        parted_kernel,
        out_shape=[
            jax.ShapeDtypeStruct((rows, 4 * wide), jnp.bfloat16),
            jax.ShapeDtypeStruct((2 * (high - rows), 2 * wide), jnp.bfloat16),
        ],
        in_specs=[pl.BlockSpec(memory_space=pltpu.SMEM)] + [vmem] * 4,
        out_specs=[vmem] * 2,
        compiler_params=pltpu.CompilerParams(vmem_limit_bytes=VMEM),
        cost_estimate=pl.CostEstimate(flops=1, bytes_accessed=1, transcendentals=0),
    )(flags, *got)


def place_kernel(flags, *refs):
    out, found = refs[-1], refs[-5:-1]
    for d, part in enumerate(found):

        @pl.when(pl.program_id(0) == d)
        def _(part=part):
            out[:, 0] = part[...].astype(out.dtype)


def placed(flags, whole, shape, found, k):
    rows = found[0].shape[0]
    before = [] if whole is None else [whole]
    return pl.pallas_call(
        place_kernel,
        grid_spec=pltpu.PrefetchScalarGridSpec(
            num_scalar_prefetch=1,
            grid=(4,),
            in_specs=[pl.BlockSpec(memory_space=pl.ANY)] * len(before)
            + [pl.BlockSpec(v.shape, lambda d, f: (0, 0, 0)) for v in found],
            out_specs=pl.BlockSpec((rows, 1) + shape[2:], lambda d, f: (k, f[MINE] ^ d, 0, 0)),
        ),
        out_shape=jax.ShapeDtypeStruct(shape, jnp.float32),
        input_output_aliases={1: 0} if before else {},
        compiler_params=pltpu.CompilerParams(vmem_limit_bytes=VMEM),
        cost_estimate=pl.CostEstimate(flops=1, bytes_accessed=1, transcendentals=0),
    )(flags, *before, *found)


def place_last_kernel(_, kept, given, out):
    out[:, 0] = kept[...] + given[...].astype(jnp.float32)


def placed_last(whole, kept, given):
    last = whole.shape[1] - 1
    block = pl.BlockSpec(given.shape, lambda i: (0, 0, 0))
    return pl.pallas_call(
        place_last_kernel,
        grid=(1,),
        in_specs=[pl.BlockSpec(memory_space=pl.ANY)] + [block] * 2,
        out_specs=pl.BlockSpec((given.shape[0], 1) + given.shape[1:], lambda i: (0, last, 0, 0)),
        out_shape=jax.ShapeDtypeStruct(whole.shape, jnp.float32),
        input_output_aliases={0: 0},
        compiler_params=pltpu.CompilerParams(vmem_limit_bytes=VMEM),
        cost_estimate=pl.CostEstimate(flops=1, bytes_accessed=1, transcendentals=0),
    )(whole, kept, given)


def shards_plane(src_real, src_imag, rcv_real, rcv_imag, src_pos, rcv_pos, freqs):
    n_z = lax.axis_size("tm")
    bins, wide, a_block = src_real.shape
    b_block = rcv_real.shape[2]
    half = wide // 2
    p_block = SRC_SL // lax.axis_size("src")
    q_plane = RCV_SL // n_z
    q_block = q_plane // 2
    q_sub = q_block // lax.axis_size("src")
    z, s, y = (lax.axis_index(name) for name in ("tm", "src", "rcv"))
    x, c = s // 2, s % 2
    mine = 2 * x + y
    last = bins - 1
    core = lambda v: lax.ppermute(v, "src", [(i, i ^ 1) for i in range(4)])
    over_x = lambda v: lax.ppermute(v, "src", [(i, i ^ 2) for i in range(4)])
    over_y = lambda v: lax.ppermute(v, "rcv", [(0, 1), (1, 0)])
    over_xy = lambda v: lax.ppermute(v, ("src", "rcv"), [(i, i ^ 5) for i in range(8)])
    over_z = lambda v, d: lax.ppermute(v, "tm", [(i, i ^ d) for i in range(n_z)])
    ends = lambda v: lax.ppermute(v, "tm", [(1, 0), (2, 3)])
    middle = lambda v: lax.ppermute(v, "tm", [(1, 2), (2, 1)])
    flat = lambda v: v.reshape(-1, v.shape[-1])
    take = lambda v, block, size: lax.dynamic_slice_in_dim(v, block * size, size)
    turn = [freqs]

    def after(v, *others):
        return lax.optimization_barrier((v, others))[0]

    def step(v):
        v = after(v, turn[0])
        turn[0] = v
        return v

    def bin_of(real, imag, which):
        return flat(jnp.stack([lax.dynamic_index_in_dim(part, which, 0, False) for part in (real, imag)]))

    def rows_of(which, first, count):
        at, size = (which, first, 0), (1, count, b_block)
        return jnp.concatenate([lax.dynamic_slice(v, at, size)[0] for v in (rcv_real, rcv_imag)], 0)

    spread = lambda got: [got[0]] + [over_z(got[d], d) for d in range(1, n_z)]
    inner = (z == 1) | (z == 2)
    flags = jnp.stack([v.astype(jnp.int32) for v in (y, c, inner, c == y, mine, x)])

    x_given = over_x(step(bin_of(src_real, src_imag, 2 * (1 - x) + y)))
    y_given = [rows_of(2 * x + 1 - y, c * half, half), rows_of(last, x * half + c * (half // 2), half // 2)]
    y_given = over_y(step(jnp.concatenate(y_given, 0)))
    raw = lax.dynamic_slice_in_dim(jnp.stack([src_real[last], src_imag[last]]), y * half, half, 1)
    raw = spread([step(flat(raw))] * n_z)
    x_own = step(bin_of(src_real, src_imag, mine))
    x_other = core(x_own)

    at_src = jnp.concatenate([take(src_pos, block, a_block) for block in (s, s ^ 2, s ^ 1, s ^ 3)])
    at_rcv = jnp.concatenate([take(rcv_pos, block, b_block) for block in (y, 1 - y)])
    f_mine, f_last = lax.dynamic_index_in_dim(freqs, mine, 0, False), freqs[last]
    chunk = p_block // CHUNKS
    here, there = s * p_block, (s ^ 2) * p_block
    n = jnp.arange(2 * p_block // FINE, dtype=jnp.int32) * FINE
    starts = jnp.where(n // chunk % 2 == 0, here, there) + n // (2 * chunk) * chunk + n % chunk
    x_other = step(x_other)
    t_source = step(tables(f_mine, starts, SRC_SL, at_src))
    x_given = step(x_given)
    x_cross = core(x_given)
    n = jnp.arange(n_z * q_block // FINE, dtype=jnp.int32) * FINE
    t_receiver = tables(f_mine, (z ^ n // q_block) * q_plane + c * q_block + n % q_block, RCV_SL, at_rcv)
    q_half = q_block // 2
    n = jnp.arange(n_z * q_half // FINE, dtype=jnp.int32) * FINE
    starts = (z ^ n // q_half) * q_plane + y * q_block + c * q_half + n % q_half
    t_receiver_last = tables(f_last, starts, RCV_SL, at_rcv)
    n = jnp.arange(2 * p_block // FINE, dtype=jnp.int32) * FINE
    starts = jnp.where(n < p_block, here, there) + n % p_block
    at_cores = jnp.concatenate([take(src_pos, block, a_block) for block in (s, s ^ 1)])
    t_source_last = tables(f_last, starts, SRC_SL, at_cores)
    t_receiver, t_receiver_last, t_source_last = step((t_receiver, t_receiver_last, t_source_last))
    y_given = step(y_given)
    y_other = core(y_given)
    x_cross, raw = step((x_cross, raw))
    raw = step(arranged(flags, raw, True))
    other_raw = over_y(raw)
    pieces = step(steered(flags, t_source, [x_own, x_given, x_other, x_cross], 4, joined=True))
    near, one = over_z(pieces, 1), middle(pieces)
    y_other = step(y_other)
    yr = receivers_of(flags, t_receiver, t_receiver_last, rcv_real, rcv_imag, y_given, y_other)
    yr, other_raw = step((yr, other_raw))
    yr = spread(yr)
    near, one, yr = step((near, one, yr))

    two, three = middle(near), ends(one)
    yr_mine, yr_last = step(parted(flags, yr, q_block))
    yr_other = core(yr_mine)
    yr_last = lax.all_gather(yr_last, "src", axis=0)
    focus_scale = 1.0 / float(wide * n_z * RCV_ST) ** 0.5
    beam_scale = 1.0 / float(SRC_ST) ** 0.5
    yr_last = step(yr_last)
    focus = step(focused(focus_scale, flags, raw, other_raw, yr_last))
    focus = step([focus, core(focus)])
    kept, given = step(steered(flags, t_source_last, focus, 2, scale=beam_scale, paired=True))
    two, three, yr_other = step((two, three, yr_other))
    given = over_x(given)
    four = [ends(two[k * 2 * chunk : (k + 1) * 2 * chunk]) for k in range(CHUNKS)]

    shape = (p_block, bins, 2, q_block)
    four[0] = step(four[0])
    parts = [pieces, near, one, three, two]
    scale = focus_scale * beam_scale
    share = lambda found: [found[0], over_y(found[1]), over_x(found[2]), over_xy(found[3])]
    found = step(product(scale, 0, 2 * chunk, flags, [*parts, four[0]], yr_mine, yr_other))
    found = share(found)
    four[1] = step(four[1])
    later = step(product(scale, 1, 2 * chunk, flags, [*parts, four[1]], yr_mine, yr_other))
    found = step(found)
    later = share(later)
    whole = step(placed(flags, None, shape, found, 0))
    given = step(given)
    whole = step(placed_last(whole, kept, given))
    later = step(later)
    return placed(flags, whole, shape, later, 1).transpose(0, 2, 1, 3)


def solution(mesh):
    plane = (mesh.shape["tm"], mesh.shape["src"], mesh.shape["rcv"]) == (4, 4, 2)
    shards = shards_plane if plane else shards_any
    in_specs = (
        P(None, "tm", "src"),
        P(None, "tm", "src"),
        P(None, "tm", "rcv"),
        P(None, "tm", "rcv"),
        P(),
        P(),
        P(),
    )
    out_specs = P("src", None, None, ("tm", "rcv"))
    return jax.shard_map(shards, mesh=mesh, in_specs=in_specs, out_specs=out_specs, check_vma=False)
```

```python
import jax
import jax.numpy as jnp
from jax import lax
from jax.experimental import pallas as pl
from jax.experimental.pallas import tpu as pltpu
from jax.sharding import PartitionSpec as P

SRC_ST = 2048
RCV_ST = 2048
SRC_SL = 2048
RCV_SL = 2048


TWO_PI = 6.283185307179586


def grid_points(first, count, total):
    index = (first + jnp.arange(count, dtype=jnp.int32)).astype(jnp.float32)
    return (2.0 * index + 1.0) / total - 1.0


def phases(freqs, slowness, positions):
    return (TWO_PI * freqs)[:, None, None] * slowness[None, :, None] * positions[None, None, :]


def mixed(form, first, second):
    return jnp.einsum(form, first, second, preferred_element_type=jnp.float32)


def receiver_fold(freqs, slow_rcv, locate, piece, start):
    part_real, part_imag = piece
    where = locate(start, part_real.shape[2])
    angle = phases(freqs, slow_rcv, where)
    steer_real = jnp.cos(angle).astype(jnp.bfloat16)
    steer_imag = jnp.sin(angle).astype(jnp.bfloat16)
    new_real = mixed("fab,fqb->faq", part_real, steer_real) - mixed(
        "fab,fqb->faq", part_imag, steer_imag
    )
    new_imag = mixed("fab,fqb->faq", part_real, steer_imag) + mixed(
        "fab,fqb->faq", part_imag, steer_real
    )
    return (new_real, new_imag)


def source_terms(freqs, slow_src, positions, focus_real, focus_imag):
    angle = phases(freqs, slow_src, positions)
    steer_real = jnp.cos(angle).astype(jnp.bfloat16)
    steer_imag = (-jnp.sin(angle)).astype(jnp.bfloat16)
    term_real = mixed("fpa,faq->pfq", steer_real, focus_real) - mixed(
        "fpa,faq->pfq", steer_imag, focus_imag
    )
    term_imag = mixed("fpa,faq->pfq", steer_real, focus_imag) + mixed(
        "fpa,faq->pfq", steer_imag, focus_real
    )
    return (term_real, term_imag)


def shards_any(src_real, src_imag, rcv_real, rcv_imag, src_pos, rcv_pos, freqs):
    n_time = lax.axis_size("tm")
    n_recv = lax.axis_size("rcv")
    n_source = lax.axis_size("src")
    src_block = src_real.shape[2]
    rcv_block = rcv_real.shape[2]
    windows = src_real.shape[1] * n_time
    q_block = RCV_SL // (n_time * n_recv)
    p_block = SRC_SL // n_source
    src_both = jnp.concatenate([src_real, src_imag], 1)
    rcv_plain = jnp.concatenate([rcv_real, rcv_imag], 1)
    rcv_turned = jnp.concatenate([-rcv_imag, rcv_real], 1)
    part_real = mixed("fwa,fwb->fab", src_both, rcv_plain)
    part_imag = mixed("fwa,fwb->fab", src_both, rcv_turned)
    q_first = (lax.axis_index("tm") * n_recv + lax.axis_index("rcv")) * q_block
    slow_rcv = grid_points(q_first, q_block, RCV_SL)
    sum_real, sum_imag = (
        lax.psum_scatter(part_real, "tm", scatter_dimension=2, tiled=True),
        lax.psum_scatter(part_imag, "tm", scatter_dimension=2, tiled=True),
    )
    sub_width = rcv_block // n_time

    def mapped(start, count):
        column = jnp.arange(count, dtype=jnp.int32)
        block = column // sub_width
        natural = block % n_recv * rcv_block + block // n_recv * sub_width + column % sub_width
        return jnp.take(rcv_pos, natural)

    cross = (sum_real.astype(jnp.bfloat16), sum_imag.astype(jnp.bfloat16))
    focus_real, focus_imag = receiver_fold(
        freqs,
        slow_rcv,
        mapped,
        (
            lax.all_gather(cross[0], ("tm", "rcv"), axis=2, tiled=True),
            lax.all_gather(cross[1], ("tm", "rcv"), axis=2, tiled=True),
        ),
        jnp.int32(0),
    )
    focus_scale = 1.0 / jnp.sqrt(jnp.float32(windows * RCV_ST))
    focus_real = (focus_real * focus_scale).astype(jnp.bfloat16)
    focus_imag = (focus_imag * focus_scale).astype(jnp.bfloat16)
    beam_scale = 1.0 / jnp.sqrt(jnp.float32(SRC_ST))
    own_pos = lax.dynamic_slice_in_dim(src_pos, lax.axis_index("src") * src_block, src_block)
    slow_src = grid_points(jnp.int32(0), p_block * lax.axis_size("src"), SRC_SL)
    term_real, term_imag = source_terms(freqs, slow_src, own_pos, focus_real, focus_imag)
    return lax.psum_scatter(
        jnp.stack([term_real, term_imag], 1) * beam_scale, "src", scatter_dimension=0, tiled=True
    )


FINE = 32
CUTS = (0, 3, 6, 8)
PLACE_Y, CORE, INNER, SAME, MINE, PLACE_X = range(6)
VMEM = 48 * 1024 * 1024


def waves(freq, slowness, positions):
    angle = ((TWO_PI * freq) * slowness)[:, None] * positions[None, :]
    return jnp.cos(angle), jnp.sin(angle)


def tables(freq, starts, total, positions):
    coarse = (2.0 * starts.astype(jnp.float32) + 1.0) / total - 1.0
    fine = 2.0 * jnp.arange(FINE, dtype=jnp.float32) / total
    return waves(freq, coarse, positions) + waves(freq, fine, positions)


def nt(first, second):
    return lax.dot_general(first, second, (((1,), (1,)), ((), ())), preferred_element_type=jnp.float32)


def steered_kernel(sign, scale, n_parts, n_halves, flags, cos_c, sin_c, cos_f, sin_f, *refs):
    parts, halves = refs[:n_parts], refs[n_parts : n_parts + n_halves]
    outs, (steer, spectra) = refs[n_parts + n_halves : -2], refs[-2:]
    step = pl.program_id(0)
    group = cos_c.shape[0]
    rows = group * FINE

    @pl.when(step == 0)
    def _():
        first = 0
        for part in parts:
            spectra[:, first : first + part.shape[1]] = part[...]
            first += part.shape[1]
        for i, part in enumerate(halves):
            count = part.shape[0] // 2
            for t in range(2):
                at = 2 * t * count + (flags[CORE] if i == 0 else 1 - flags[CORE]) * count
                spectra[pl.ds(pl.multiple_of(at, count), count), first:] = part[t * count : (t + 1) * count, :]

    for i in range(group):
        cc, sc = cos_c[i : i + 1, :], sin_c[i : i + 1, :]
        steer[i * FINE : (i + 1) * FINE, :] = (cc * cos_f[...] - sc * sin_f[...]).astype(jnp.bfloat16)
        steer[rows + i * FINE : rows + (i + 1) * FINE, :] = (sc * cos_f[...] + cc * sin_f[...]).astype(
            jnp.bfloat16
        )
    found = nt(steer[...], spectra[...])
    half = found.shape[1] // 2
    real = (found[:rows, :half] + found[rows:, half:]) * scale
    imag = (found[:rows, half:] - found[rows:, :half]) * (sign * scale)
    for k, out in enumerate(outs):

        size = out.shape[0]
        per = rows // size

        @pl.when((step == k // per) | (len(outs) == 1))
        def _(out=out, at=k % per * size):
            if out.ndim == 2:
                out[:, :half] = real[at : at + size].astype(out.dtype)
                out[:, half:] = imag[at : at + size].astype(out.dtype)
            else:
                out[:, 0, :] = real.astype(out.dtype)
                out[:, 1, :] = imag.astype(out.dtype)


def steered(flags, table, parts, steps, halves=(), cuts=1, sign=1.0, scale=1.0, paired=False, joined=False):
    coarse, depth = table[0].shape
    wide = parts[0].shape[0]
    group = coarse // steps
    rows = group * FINE
    whole = lambda v: pl.BlockSpec(v.shape, lambda i: (0, 0))
    if paired:
        shape, spec = jax.ShapeDtypeStruct((rows, 2, wide // 2), jnp.float32), pl.BlockSpec(
            (rows, 2, wide // 2), lambda i: (0, 0, 0)
        )
    else:
        shape, spec = jax.ShapeDtypeStruct((rows, wide), jnp.bfloat16), pl.BlockSpec((rows, wide), lambda i: (0, 0))
    shapes, specs = [shape] * steps, [spec] * steps
    if paired:
        shapes[1:] = [jax.ShapeDtypeStruct(shape.shape, jnp.bfloat16)] * (steps - 1)
    if cuts > 1:
        shapes = [jax.ShapeDtypeStruct((rows // cuts, wide), jnp.bfloat16)] * (steps * cuts)
        specs = [pl.BlockSpec((rows // cuts, wide), lambda i: (0, 0))] * (steps * cuts)
    if joined:
        shapes = jax.ShapeDtypeStruct((steps * rows, wide), jnp.bfloat16)
        specs = pl.BlockSpec((rows, wide), lambda i: (i, 0))
    return pl.pallas_call(
        lambda *refs: steered_kernel(sign, scale, len(parts), len(halves), *refs),
        grid=(steps,),
        in_specs=[pl.BlockSpec(memory_space=pltpu.SMEM)]
        + [pl.BlockSpec((group, depth), lambda i: (i, 0))] * 2
        + [whole(v) for v in (*table[2:], *parts, *halves)],
        out_specs=specs,
        out_shape=shapes,
        scratch_shapes=[pltpu.VMEM((2 * rows, depth), jnp.bfloat16), pltpu.VMEM((wide, depth), jnp.bfloat16)],
        compiler_params=pltpu.CompilerParams(vmem_limit_bytes=VMEM),
        cost_estimate=pl.CostEstimate(flops=1, bytes_accessed=1, transcendentals=0),
    )(flags, *table, *parts, *halves)


def focus_kernel(scale, flags, slots, others, receiver, out, real, imag, both):
    n_z, rows, _ = slots.shape
    half = rows // 2
    wide = rows
    part = receiver.shape[1]
    q = 2 * part
    for slot in range(n_z):
        for v, at in ((slots, flags[PLACE_Y] * half), (others, (1 - flags[PLACE_Y]) * half)):
            to = pl.ds(pl.multiple_of(slot * wide + at, half), half)
            real[to, :] = v[slot, :half, :]
            imag[to, :] = v[slot, half:, :]
        for t in range(2):
            for i in range(receiver.shape[0]):
                row, col = t * q + i % 2 * part, slot * wide + i // 2 * half
                both[row : row + part, col : col + half] = receiver[i, :, (2 * slot + t) * half : (2 * slot + t + 1) * half]
    one = jnp.dot(both[...], real[...], preferred_element_type=jnp.float32)
    two = jnp.dot(both[...], imag[...], preferred_element_type=jnp.float32)
    out[:q, :] = ((one[:q] - two[q:]) * scale).astype(out.dtype)
    out[q:, :] = ((one[q:] + two[:q]) * scale).astype(out.dtype)


def focused(scale, flags, slots, others, receiver):
    n_z, rows, stations = slots.shape
    q = 2 * receiver.shape[1]
    vmem = pl.BlockSpec(memory_space=pltpu.VMEM)
    return pl.pallas_call(
        lambda *refs: focus_kernel(scale, *refs),
        out_shape=jax.ShapeDtypeStruct((2 * q, stations), jnp.bfloat16),
        in_specs=[pl.BlockSpec(memory_space=pltpu.SMEM)] + [vmem] * 3,
        out_specs=vmem,
        scratch_shapes=[pltpu.VMEM((n_z * rows, stations), jnp.bfloat16)] * 2
        + [pltpu.VMEM((2 * q, n_z * rows), jnp.bfloat16)],
        compiler_params=pltpu.CompilerParams(vmem_limit_bytes=VMEM),
        cost_estimate=pl.CostEstimate(flops=1, bytes_accessed=1, transcendentals=0),
    )(flags, slots, others, receiver)


def product_kernel(scale, flags, own, near, one, two, three, four, mine, other, *refs):
    outs, both = refs[:-1], refs[-1]
    rows = both.shape[0] // 2
    wide = own.shape[1]
    half = wide // 2
    for slot, part in enumerate((own[...], near[...], one[...] + two[...], three[...] + four[...])):
        at = slot * wide
        real, imag = part[:, :half], part[:, half:]
        both[:rows, at : at + half] = real
        both[:rows, at + half : at + wide] = -imag
        both[rows:, at : at + half] = imag
        both[rows:, at + half : at + wide] = real
    middle = rows // 2
    same = flags[SAME] == 1
    by_mine, by_other = nt(both[...], mine[...]) * scale, nt(both[...], other[...]) * scale
    for total, one, two in (
        (jnp.where(same, by_mine, by_other), outs[0], outs[2]),
        (jnp.where(same, by_other, by_mine), outs[1], outs[3]),
    ):
        for t in range(2):
            one[:, t, :] = total[t * rows : t * rows + middle].astype(one.dtype)
            two[:, t, :] = total[t * rows + middle : (t + 1) * rows].astype(two.dtype)


def product(scale, k, rows, flags, parts, mine, other):
    shape = (rows // 2, 2, mine.shape[0])
    return pl.pallas_call(
        lambda *refs: product_kernel(scale, *refs),
        grid=(1,),
        out_shape=[jax.ShapeDtypeStruct(shape, kind) for kind in (jnp.float32,) + (jnp.bfloat16,) * 3],
        in_specs=[pl.BlockSpec(memory_space=pltpu.SMEM)]
        + [pl.BlockSpec((rows, v.shape[1]), lambda i: (k, 0)) for v in parts[:-1]]
        + [pl.BlockSpec(v.shape, lambda i: (0, 0)) for v in (parts[-1], mine, other)],
        out_specs=[pl.BlockSpec(shape, lambda i: (0, 0, 0))] * 4,
        scratch_shapes=[pltpu.VMEM((2 * rows, mine.shape[1]), jnp.bfloat16)],
        compiler_params=pltpu.CompilerParams(vmem_limit_bytes=VMEM),
        cost_estimate=pl.CostEstimate(flops=1, bytes_accessed=1, transcendentals=0),
    )(flags, *parts, mine, other)


def arranged_kernel(flags, own, one, two, three, out):
    inner = flags[INNER] == 1
    second, third = jnp.where(inner, three[...], two[...]), jnp.where(inner, two[...], three[...])
    wide = own.shape[1]
    for slot, v in enumerate((own[...], one[...], second, third)):
        if out.ndim == 3:
            out[slot] = v
        else:
            out[:, slot * wide : (slot + 1) * wide] = v


def arranged(flags, got, stacked):
    rows, wide = got[0].shape
    vmem = pl.BlockSpec(memory_space=pltpu.VMEM)
    return pl.pallas_call(
        arranged_kernel,
        out_shape=jax.ShapeDtypeStruct((4, rows, wide) if stacked else (rows, 4 * wide), got[0].dtype),
        in_specs=[pl.BlockSpec(memory_space=pltpu.SMEM)] + [vmem] * 4,
        out_specs=vmem,
        compiler_params=pltpu.CompilerParams(vmem_limit_bytes=VMEM),
        cost_estimate=pl.CostEstimate(flops=1, bytes_accessed=1, transcendentals=0),
    )(flags, *got)


def fill_steering(steer, cos_c, sin_c, cos_f, sin_f, first, count):
    for i in range(count):
        cc, sc = cos_c[pl.ds(first + i, 1), :], sin_c[pl.ds(first + i, 1), :]
        steer[i * FINE : (i + 1) * FINE, :] = (cc * cos_f[...] - sc * sin_f[...]).astype(steer.dtype)
        steer[(count + i) * FINE : (count + i + 1) * FINE, :] = (sc * cos_f[...] + cc * sin_f[...]).astype(
            steer.dtype
        )


def conjugated(steer, spectra):
    found = nt(steer[...], spectra[...])
    rows, half = found.shape[0] // 2, found.shape[1] // 2
    return found[:rows, :half] + found[rows:, half:], found[rows:, :half] - found[:rows, half:]


def receivers_kernel(flags, *refs):
    tables, own, own_last, (given, other) = (refs[:4], refs[4:8]), refs[8:10], refs[10:12], refs[12:14]
    outs, (steer, spectra, steer_last, spectra_last) = refs[14:-4], refs[-4:]
    step = pl.program_id(0)

    @pl.when(step == 0)
    def _():
        first = 0
        for to, here in ((spectra, own), (spectra_last, own_last)):
            b_block, count = here[0].shape[2], here[0].shape[1] // 2
            to[: 2 * count, :b_block] = here[0][0]
            to[2 * count :, :b_block] = here[1][0]
            for t in range(2):
                rows = slice(first + t * count, first + (t + 1) * count)
                for part, place in ((given, flags[CORE]), (other, 1 - flags[CORE])):
                    at = pl.multiple_of((2 * t + place) * count, count)
                    to[pl.ds(at, count), b_block:] = part[rows, :]
            first += 2 * count

    coarse = tables[0][0].shape[0]
    fill_steering(steer, *tables[0], 0, coarse)
    real, imag = conjugated(steer, spectra)
    coarse_last = tables[1][0].shape[0] // len(outs)
    fill_steering(steer_last, *tables[1], step * coarse_last, coarse_last)
    real_last, imag_last = conjugated(steer_last, spectra_last)
    rows, wide = real.shape
    half, part = real_last.shape[0] // 2, wide // 2
    for k, out in enumerate(outs):

        @pl.when(step == k)
        def _(out=out):
            out[:rows, :wide] = real.astype(out.dtype)
            out[:rows, wide:] = imag.astype(out.dtype)
            for i in range(2):
                at = slice(i * half, (i + 1) * half)
                out[rows:, 2 * i * part : (2 * i + 1) * part] = real_last[at].astype(out.dtype)
                out[rows:, (2 * i + 1) * part : (2 * i + 2) * part] = imag_last[at].astype(out.dtype)


def receivers_of(flags, table, table_last, real, imag, given, other):
    planes = 4
    bins, wide, b_block = real.shape
    coarse, depth = table[0].shape
    rows, rows_last = coarse * FINE // planes, table_last[0].shape[0] * FINE // planes
    shape = jax.ShapeDtypeStruct((rows + rows_last // 2, 2 * wide), jnp.bfloat16)
    whole = lambda v: pl.BlockSpec(v.shape, lambda i, f: (0, 0))
    return pl.pallas_call(
        receivers_kernel,
        grid_spec=pltpu.PrefetchScalarGridSpec(
            num_scalar_prefetch=1,
            grid=(planes,),
            in_specs=[pl.BlockSpec((coarse // planes, depth), lambda i, f: (i, 0))] * 2
            + [whole(v) for v in (*table[2:], *table_last)]
            + [pl.BlockSpec((1, wide, b_block), lambda i, f: (f[MINE], 0, 0))] * 2
            + [pl.BlockSpec((1, wide // 2, b_block), lambda i, f: (bins - 1, f[PLACE_X], 0))] * 2
            + [whole(given), whole(other)],
            out_specs=[pl.BlockSpec(shape.shape, lambda i, f: (0, 0))] * planes,
            scratch_shapes=[
                pltpu.VMEM((2 * rows, depth), jnp.bfloat16),
                pltpu.VMEM((2 * wide, depth), jnp.bfloat16),
                pltpu.VMEM((2 * rows_last, depth), jnp.bfloat16),
                pltpu.VMEM((wide, depth), jnp.bfloat16),
            ],
        ),
        out_shape=[shape] * planes,
        compiler_params=pltpu.CompilerParams(vmem_limit_bytes=VMEM),
        cost_estimate=pl.CostEstimate(flops=1, bytes_accessed=1, transcendentals=0),
    )(flags, *table, *table_last, real, imag, real, imag, given, other)


def parted_kernel(flags, own, one, two, three, out, out_last):
    inner = flags[INNER] == 1
    second, third = jnp.where(inner, three[...], two[...]), jnp.where(inner, two[...], three[...])
    wide, half, rows = own.shape[1], own.shape[1] // 2, out.shape[0]
    rest = own.shape[0] - rows
    for slot, v in enumerate((own[...], one[...], second, third)):
        out[:, slot * wide : (slot + 1) * wide] = v[:rows]
        for i in range(2):
            out_last[i * rest : (i + 1) * rest, slot * half : (slot + 1) * half] = v[rows:, i * half : (i + 1) * half]


def parted(flags, got, rows):
    vmem = pl.BlockSpec(memory_space=pltpu.VMEM)
    high, wide = got[0].shape
    return pl.pallas_call(
        parted_kernel,
        out_shape=[
            jax.ShapeDtypeStruct((rows, 4 * wide), jnp.bfloat16),
            jax.ShapeDtypeStruct((2 * (high - rows), 2 * wide), jnp.bfloat16),
        ],
        in_specs=[pl.BlockSpec(memory_space=pltpu.SMEM)] + [vmem] * 4,
        out_specs=[vmem] * 2,
        compiler_params=pltpu.CompilerParams(vmem_limit_bytes=VMEM),
        cost_estimate=pl.CostEstimate(flops=1, bytes_accessed=1, transcendentals=0),
    )(flags, *got)


def place_kernel(flags, *refs):
    out, found = refs[-1], refs[-5:-1]
    for d, part in enumerate(found):

        @pl.when(pl.program_id(0) == d)
        def _(part=part):
            out[:, 0] = part[...].astype(out.dtype)


def placed(flags, whole, shape, found, k):
    rows = found[0].shape[0]
    before = [] if whole is None else [whole]
    return pl.pallas_call(
        place_kernel,
        grid_spec=pltpu.PrefetchScalarGridSpec(
            num_scalar_prefetch=1,
            grid=(4,),
            in_specs=[pl.BlockSpec(memory_space=pl.ANY)] * len(before)
            + [pl.BlockSpec(v.shape, lambda d, f: (0, 0, 0)) for v in found],
            out_specs=pl.BlockSpec((rows, 1) + shape[2:], lambda d, f: (k, f[MINE] ^ d, 0, 0)),
        ),
        out_shape=jax.ShapeDtypeStruct(shape, jnp.float32),
        input_output_aliases={1: 0} if before else {},
        compiler_params=pltpu.CompilerParams(vmem_limit_bytes=VMEM),
        cost_estimate=pl.CostEstimate(flops=1, bytes_accessed=1, transcendentals=0),
    )(flags, *before, *found)


def place_last_kernel(_, kept, given, out):
    out[:, 0] = kept[...] + given[...].astype(jnp.float32)


def placed_last(whole, kept, given):
    last = whole.shape[1] - 1
    block = pl.BlockSpec(given.shape, lambda i: (0, 0, 0))
    return pl.pallas_call(
        place_last_kernel,
        grid=(1,),
        in_specs=[pl.BlockSpec(memory_space=pl.ANY)] + [block] * 2,
        out_specs=pl.BlockSpec((given.shape[0], 1) + given.shape[1:], lambda i: (0, last, 0, 0)),
        out_shape=jax.ShapeDtypeStruct(whole.shape, jnp.float32),
        input_output_aliases={0: 0},
        compiler_params=pltpu.CompilerParams(vmem_limit_bytes=VMEM),
        cost_estimate=pl.CostEstimate(flops=1, bytes_accessed=1, transcendentals=0),
    )(whole, kept, given)


def shards_plane(src_real, src_imag, rcv_real, rcv_imag, src_pos, rcv_pos, freqs):
    n_z = lax.axis_size("tm")
    bins, wide, a_block = src_real.shape
    b_block = rcv_real.shape[2]
    half = wide // 2
    p_block = SRC_SL // lax.axis_size("src")
    q_plane = RCV_SL // n_z
    q_block = q_plane // 2
    q_sub = q_block // lax.axis_size("src")
    z, s, y = (lax.axis_index(name) for name in ("tm", "src", "rcv"))
    x, c = s // 2, s % 2
    mine = 2 * x + y
    last = bins - 1
    core = lambda v: lax.ppermute(v, "src", [(i, i ^ 1) for i in range(4)])
    over_x = lambda v: lax.ppermute(v, "src", [(i, i ^ 2) for i in range(4)])
    over_y = lambda v: lax.ppermute(v, "rcv", [(0, 1), (1, 0)])
    over_xy = lambda v: lax.ppermute(v, ("src", "rcv"), [(i, i ^ 5) for i in range(8)])
    over_z = lambda v, d: lax.ppermute(v, "tm", [(i, i ^ d) for i in range(n_z)])
    ends = lambda v: lax.ppermute(v, "tm", [(1, 0), (2, 3)])
    middle = lambda v: lax.ppermute(v, "tm", [(1, 2), (2, 1)])
    flat = lambda v: v.reshape(-1, v.shape[-1])
    take = lambda v, block, size: lax.dynamic_slice_in_dim(v, block * size, size)
    turn = [freqs]

    def after(v, *others):
        return lax.optimization_barrier((v, others))[0]

    def step(v):
        v = after(v, turn[0])
        turn[0] = v
        return v

    def bin_of(real, imag, which):
        return flat(jnp.stack([lax.dynamic_index_in_dim(part, which, 0, False) for part in (real, imag)]))

    def rows_of(which, first, count):
        at, size = (which, first, 0), (1, count, b_block)
        return jnp.concatenate([lax.dynamic_slice(v, at, size)[0] for v in (rcv_real, rcv_imag)], 0)

    spread = lambda got: [got[0]] + [over_z(got[d], d) for d in range(1, n_z)]
    inner = (z == 1) | (z == 2)
    flags = jnp.stack([v.astype(jnp.int32) for v in (y, c, inner, c == y, mine, x)])

    x_given = over_x(step(bin_of(src_real, src_imag, 2 * (1 - x) + y)))
    y_given = [rows_of(2 * x + 1 - y, c * half, half), rows_of(last, x * half + c * (half // 2), half // 2)]
    y_given = over_y(step(jnp.concatenate(y_given, 0)))
    raw = lax.dynamic_slice_in_dim(jnp.stack([src_real[last], src_imag[last]]), y * half, half, 1)
    raw = spread([step(flat(raw))] * n_z)
    x_own = step(bin_of(src_real, src_imag, mine))
    raw[1], x_own = step((raw[1], x_own))
    x_other = core(x_own)

    at_src = jnp.concatenate([take(src_pos, block, a_block) for block in (s, s ^ 2, s ^ 1, s ^ 3)])
    at_rcv = jnp.concatenate([take(rcv_pos, block, b_block) for block in (y, 1 - y)])
    f_mine, f_last = lax.dynamic_index_in_dim(freqs, mine, 0, False), freqs[last]
    here, there = s * p_block, (s ^ 2) * p_block
    cuts = [cut * p_block // CUTS[-1] for cut in CUTS]
    spans = list(zip(cuts, cuts[1:]))
    runs = [(i, n) for span in spans for i in range(2) for n in range(*span, FINE)]
    side, first = jnp.array([i for i, _ in runs], jnp.int32), jnp.array([n for _, n in runs], jnp.int32)
    starts = jnp.where(side == 0, here, there) + first
    t_source = step(tables(f_mine, starts, SRC_SL, at_src))
    x_given = step(x_given)
    x_cross = core(x_given)
    n = jnp.arange(n_z * q_block // FINE, dtype=jnp.int32) * FINE
    t_receiver = tables(f_mine, (z ^ n // q_block) * q_plane + c * q_block + n % q_block, RCV_SL, at_rcv)
    q_half = q_block // 2
    n = jnp.arange(n_z * q_half // FINE, dtype=jnp.int32) * FINE
    starts = (z ^ n // q_half) * q_plane + y * q_block + c * q_half + n % q_half
    t_receiver_last = tables(f_last, starts, RCV_SL, at_rcv)
    n = jnp.arange(2 * p_block // FINE, dtype=jnp.int32) * FINE
    starts = jnp.where(n < p_block, here, there) + n % p_block
    at_cores = jnp.concatenate([take(src_pos, block, a_block) for block in (s, s ^ 1)])
    t_source_last = tables(f_last, starts, SRC_SL, at_cores)
    t_receiver, t_receiver_last, t_source_last = step((t_receiver, t_receiver_last, t_source_last))
    y_given = step(y_given)
    y_other = core(y_given)
    x_cross, x_other, raw = step((x_cross, x_other, raw))
    raw = step(arranged(flags, raw, True))
    other_raw = over_y(raw)
    pieces = step(steered(flags, t_source, [x_own, x_given, x_other, x_cross], 4, joined=True))
    near, one = over_z(pieces, 1), middle(pieces)
    y_other = step(y_other)
    yr = receivers_of(flags, t_receiver, t_receiver_last, rcv_real, rcv_imag, y_given, y_other)
    yr, other_raw = step((yr, other_raw))
    yr = spread(yr)
    near, one, yr = step((near, one, yr))

    two, three = middle(near), ends(one)
    yr_mine, yr_last = step(parted(flags, yr, q_block))
    yr_other = core(yr_mine)
    yr_last = lax.all_gather(yr_last, "src", axis=0)
    focus_scale = 1.0 / float(wide * n_z * RCV_ST) ** 0.5
    beam_scale = 1.0 / float(SRC_ST) ** 0.5
    yr_last = step(yr_last)
    focus = step(focused(focus_scale, flags, raw, other_raw, yr_last))
    focus = step([focus, core(focus)])
    two, three, yr_other = step((two, three, yr_other))
    four = [ends(two[2 * first : 2 * past]) for first, past in spans]
    kept, given = step(steered(flags, t_source_last, focus, 2, scale=beam_scale, paired=True))
    given = over_x(given)
    shape = (p_block, bins, 2, q_block)
    parts = [pieces, near, one, three, two]
    scale = focus_scale * beam_scale
    sent, whole = [], None
    for k, (first, past) in enumerate(spans):
        rows = 2 * (past - first)
        four[k] = step(four[k])
        found = step(product(scale, 2 * first // rows, rows, flags, [*parts, four[k]], yr_mine, yr_other))
        if k == 0:
            given = step(given)
        if k > 0:
            sent[-1] = step(sent[-1])
        sent.append([found[0], over_y(found[1]), over_x(found[2]), over_xy(found[3])])
    for k, (first, past) in enumerate(spans):
        found = step(sent[k]) if k == len(spans) - 1 else sent[k]
        whole = placed(flags, whole, shape, found, first // (past - first))
        if k == 0:
            whole = placed_last(whole, kept, given)
    return whole.transpose(0, 2, 1, 3)


def solution(mesh):
    plane = (mesh.shape["tm"], mesh.shape["src"], mesh.shape["rcv"]) == (4, 4, 2)
    shards = shards_plane if plane else shards_any
    in_specs = (
        P(None, "tm", "src"),
        P(None, "tm", "src"),
        P(None, "tm", "rcv"),
        P(None, "tm", "rcv"),
        P(),
        P(),
        P(),
    )
    out_specs = P("src", None, None, ("tm", "rcv"))
    return jax.shard_map(shards, mesh=mesh, in_specs=in_specs, out_specs=out_specs, check_vma=False)
```

```python
import jax
import jax.numpy as jnp
from jax import lax
from jax.experimental import pallas as pl
from jax.experimental.pallas import tpu as pltpu
from jax.sharding import PartitionSpec as P

SRC_ST = 2048
RCV_ST = 2048
SRC_SL = 2048
RCV_SL = 2048


TWO_PI = 6.283185307179586


def grid_points(first, count, total):
    index = (first + jnp.arange(count, dtype=jnp.int32)).astype(jnp.float32)
    return (2.0 * index + 1.0) / total - 1.0


def phases(freqs, slowness, positions):
    return (TWO_PI * freqs)[:, None, None] * slowness[None, :, None] * positions[None, None, :]


def mixed(form, first, second):
    return jnp.einsum(form, first, second, preferred_element_type=jnp.float32)


def receiver_fold(freqs, slow_rcv, locate, piece, start):
    part_real, part_imag = piece
    where = locate(start, part_real.shape[2])
    angle = phases(freqs, slow_rcv, where)
    steer_real = jnp.cos(angle).astype(jnp.bfloat16)
    steer_imag = jnp.sin(angle).astype(jnp.bfloat16)
    new_real = mixed("fab,fqb->faq", part_real, steer_real) - mixed(
        "fab,fqb->faq", part_imag, steer_imag
    )
    new_imag = mixed("fab,fqb->faq", part_real, steer_imag) + mixed(
        "fab,fqb->faq", part_imag, steer_real
    )
    return (new_real, new_imag)


def source_terms(freqs, slow_src, positions, focus_real, focus_imag):
    angle = phases(freqs, slow_src, positions)
    steer_real = jnp.cos(angle).astype(jnp.bfloat16)
    steer_imag = (-jnp.sin(angle)).astype(jnp.bfloat16)
    term_real = mixed("fpa,faq->pfq", steer_real, focus_real) - mixed(
        "fpa,faq->pfq", steer_imag, focus_imag
    )
    term_imag = mixed("fpa,faq->pfq", steer_real, focus_imag) + mixed(
        "fpa,faq->pfq", steer_imag, focus_real
    )
    return (term_real, term_imag)


def shards_any(src_real, src_imag, rcv_real, rcv_imag, src_pos, rcv_pos, freqs):
    n_time = lax.axis_size("tm")
    n_recv = lax.axis_size("rcv")
    n_source = lax.axis_size("src")
    src_block = src_real.shape[2]
    rcv_block = rcv_real.shape[2]
    windows = src_real.shape[1] * n_time
    q_block = RCV_SL // (n_time * n_recv)
    p_block = SRC_SL // n_source
    src_both = jnp.concatenate([src_real, src_imag], 1)
    rcv_plain = jnp.concatenate([rcv_real, rcv_imag], 1)
    rcv_turned = jnp.concatenate([-rcv_imag, rcv_real], 1)
    part_real = mixed("fwa,fwb->fab", src_both, rcv_plain)
    part_imag = mixed("fwa,fwb->fab", src_both, rcv_turned)
    q_first = (lax.axis_index("tm") * n_recv + lax.axis_index("rcv")) * q_block
    slow_rcv = grid_points(q_first, q_block, RCV_SL)
    sum_real, sum_imag = (
        lax.psum_scatter(part_real, "tm", scatter_dimension=2, tiled=True),
        lax.psum_scatter(part_imag, "tm", scatter_dimension=2, tiled=True),
    )
    sub_width = rcv_block // n_time

    def mapped(start, count):
        column = jnp.arange(count, dtype=jnp.int32)
        block = column // sub_width
        natural = block % n_recv * rcv_block + block // n_recv * sub_width + column % sub_width
        return jnp.take(rcv_pos, natural)

    cross = (sum_real.astype(jnp.bfloat16), sum_imag.astype(jnp.bfloat16))
    focus_real, focus_imag = receiver_fold(
        freqs,
        slow_rcv,
        mapped,
        (
            lax.all_gather(cross[0], ("tm", "rcv"), axis=2, tiled=True),
            lax.all_gather(cross[1], ("tm", "rcv"), axis=2, tiled=True),
        ),
        jnp.int32(0),
    )
    focus_scale = 1.0 / jnp.sqrt(jnp.float32(windows * RCV_ST))
    focus_real = (focus_real * focus_scale).astype(jnp.bfloat16)
    focus_imag = (focus_imag * focus_scale).astype(jnp.bfloat16)
    beam_scale = 1.0 / jnp.sqrt(jnp.float32(SRC_ST))
    own_pos = lax.dynamic_slice_in_dim(src_pos, lax.axis_index("src") * src_block, src_block)
    slow_src = grid_points(jnp.int32(0), p_block * lax.axis_size("src"), SRC_SL)
    term_real, term_imag = source_terms(freqs, slow_src, own_pos, focus_real, focus_imag)
    return lax.psum_scatter(
        jnp.stack([term_real, term_imag], 1) * beam_scale, "src", scatter_dimension=0, tiled=True
    )


FINE = 32
CUTS = (0, 3, 6, 8)
PLACE_Y, CORE, INNER, SAME, MINE, PLACE_X = range(6)
VMEM = 48 * 1024 * 1024


def waves(freq, slowness, positions):
    angle = ((TWO_PI * freq) * slowness)[:, None] * positions[None, :]
    return jnp.cos(angle), jnp.sin(angle)


def tables(freq, starts, total, positions):
    coarse = (2.0 * starts.astype(jnp.float32) + 1.0) / total - 1.0
    fine = 2.0 * jnp.arange(FINE, dtype=jnp.float32) / total
    return waves(freq, coarse, positions) + waves(freq, fine, positions)


def nt(first, second):
    return lax.dot_general(first, second, (((1,), (1,)), ((), ())), preferred_element_type=jnp.float32)


def steered_kernel(sign, scale, n_parts, n_halves, flags, cos_c, sin_c, cos_f, sin_f, *refs):
    parts, halves = refs[:n_parts], refs[n_parts : n_parts + n_halves]
    outs, (steer, spectra) = refs[n_parts + n_halves : -2], refs[-2:]
    step = pl.program_id(0)
    group = cos_c.shape[0]
    rows = group * FINE

    @pl.when(step == 0)
    def _():
        first = 0
        for part in parts:
            spectra[:, first : first + part.shape[1]] = part[...]
            first += part.shape[1]
        for i, part in enumerate(halves):
            count = part.shape[0] // 2
            for t in range(2):
                at = 2 * t * count + (flags[CORE] if i == 0 else 1 - flags[CORE]) * count
                spectra[pl.ds(pl.multiple_of(at, count), count), first:] = part[t * count : (t + 1) * count, :]

    for i in range(group):
        cc, sc = cos_c[i : i + 1, :], sin_c[i : i + 1, :]
        steer[i * FINE : (i + 1) * FINE, :] = (cc * cos_f[...] - sc * sin_f[...]).astype(jnp.bfloat16)
        steer[rows + i * FINE : rows + (i + 1) * FINE, :] = (sc * cos_f[...] + cc * sin_f[...]).astype(
            jnp.bfloat16
        )
    found = nt(steer[...], spectra[...])
    half = found.shape[1] // 2
    real = (found[:rows, :half] + found[rows:, half:]) * scale
    imag = (found[:rows, half:] - found[rows:, :half]) * (sign * scale)
    for k, out in enumerate(outs):

        size = out.shape[0]
        per = rows // size

        @pl.when((step == k // per) | (len(outs) == 1))
        def _(out=out, at=k % per * size):
            if out.ndim == 2:
                out[:, :half] = real[at : at + size].astype(out.dtype)
                out[:, half:] = imag[at : at + size].astype(out.dtype)
            else:
                out[:, 0, :] = real.astype(out.dtype)
                out[:, 1, :] = imag.astype(out.dtype)


def steered(flags, table, parts, steps, halves=(), cuts=1, sign=1.0, scale=1.0, paired=False, joined=False):
    coarse, depth = table[0].shape
    wide = parts[0].shape[0]
    group = coarse // steps
    rows = group * FINE
    whole = lambda v: pl.BlockSpec(v.shape, lambda i: (0, 0))
    if paired:
        shape, spec = jax.ShapeDtypeStruct((rows, 2, wide // 2), jnp.float32), pl.BlockSpec(
            (rows, 2, wide // 2), lambda i: (0, 0, 0)
        )
    else:
        shape, spec = jax.ShapeDtypeStruct((rows, wide), jnp.bfloat16), pl.BlockSpec((rows, wide), lambda i: (0, 0))
    shapes, specs = [shape] * steps, [spec] * steps
    if paired:
        shapes[1:] = [jax.ShapeDtypeStruct(shape.shape, jnp.bfloat16)] * (steps - 1)
    if cuts > 1:
        shapes = [jax.ShapeDtypeStruct((rows // cuts, wide), jnp.bfloat16)] * (steps * cuts)
        specs = [pl.BlockSpec((rows // cuts, wide), lambda i: (0, 0))] * (steps * cuts)
    if joined:
        shapes = jax.ShapeDtypeStruct((steps * rows, wide), jnp.bfloat16)
        specs = pl.BlockSpec((rows, wide), lambda i: (i, 0))
    return pl.pallas_call(
        lambda *refs: steered_kernel(sign, scale, len(parts), len(halves), *refs),
        grid=(steps,),
        in_specs=[pl.BlockSpec(memory_space=pltpu.SMEM)]
        + [pl.BlockSpec((group, depth), lambda i: (i, 0))] * 2
        + [whole(v) for v in (*table[2:], *parts, *halves)],
        out_specs=specs,
        out_shape=shapes,
        scratch_shapes=[pltpu.VMEM((2 * rows, depth), jnp.bfloat16), pltpu.VMEM((wide, depth), jnp.bfloat16)],
        compiler_params=pltpu.CompilerParams(vmem_limit_bytes=VMEM),
        cost_estimate=pl.CostEstimate(flops=1, bytes_accessed=1, transcendentals=0),
    )(flags, *table, *parts, *halves)


def focus_kernel(scale, flags, slots, others, receiver, out, real, imag, both):
    n_z, rows, _ = slots.shape
    half = rows // 2
    wide = rows
    part = receiver.shape[1]
    q = 2 * part
    for slot in range(n_z):
        for v, at in ((slots, flags[PLACE_Y] * half), (others, (1 - flags[PLACE_Y]) * half)):
            to = pl.ds(pl.multiple_of(slot * wide + at, half), half)
            real[to, :] = v[slot, :half, :]
            imag[to, :] = v[slot, half:, :]
        for t in range(2):
            for i in range(receiver.shape[0]):
                row, col = t * q + i % 2 * part, slot * wide + i // 2 * half
                both[row : row + part, col : col + half] = receiver[i, :, (2 * slot + t) * half : (2 * slot + t + 1) * half]
    one = jnp.dot(both[...], real[...], preferred_element_type=jnp.float32)
    two = jnp.dot(both[...], imag[...], preferred_element_type=jnp.float32)
    out[:q, :] = ((one[:q] - two[q:]) * scale).astype(out.dtype)
    out[q:, :] = ((one[q:] + two[:q]) * scale).astype(out.dtype)


def focused(scale, flags, slots, others, receiver):
    n_z, rows, stations = slots.shape
    q = 2 * receiver.shape[1]
    vmem = pl.BlockSpec(memory_space=pltpu.VMEM)
    return pl.pallas_call(
        lambda *refs: focus_kernel(scale, *refs),
        out_shape=jax.ShapeDtypeStruct((2 * q, stations), jnp.bfloat16),
        in_specs=[pl.BlockSpec(memory_space=pltpu.SMEM)] + [vmem] * 3,
        out_specs=vmem,
        scratch_shapes=[pltpu.VMEM((n_z * rows, stations), jnp.bfloat16)] * 2
        + [pltpu.VMEM((2 * q, n_z * rows), jnp.bfloat16)],
        compiler_params=pltpu.CompilerParams(vmem_limit_bytes=VMEM),
        cost_estimate=pl.CostEstimate(flops=1, bytes_accessed=1, transcendentals=0),
    )(flags, slots, others, receiver)


def product_kernel(scale, flags, own, near, one, two, three, four, mine, other, *refs):
    outs, both = refs[:-1], refs[-1]
    rows = both.shape[0] // 2
    wide = own.shape[1]
    half = wide // 2
    for slot, part in enumerate((own[...], near[...], one[...] + two[...], three[...] + four[...])):
        at = slot * wide
        real, imag = part[:, :half], part[:, half:]
        both[:rows, at : at + half] = real
        both[:rows, at + half : at + wide] = -imag
        both[rows:, at : at + half] = imag
        both[rows:, at + half : at + wide] = real
    middle = rows // 2
    same = flags[SAME] == 1
    by_mine, by_other = nt(both[...], mine[...]) * scale, nt(both[...], other[...]) * scale
    for total, one, two in (
        (jnp.where(same, by_mine, by_other), outs[0], outs[2]),
        (jnp.where(same, by_other, by_mine), outs[1], outs[3]),
    ):
        for t in range(2):
            one[:, t, :] = total[t * rows : t * rows + middle].astype(one.dtype)
            two[:, t, :] = total[t * rows + middle : (t + 1) * rows].astype(two.dtype)


def product(scale, k, rows, flags, parts, mine, other):
    shape = (rows // 2, 2, mine.shape[0])
    return pl.pallas_call(
        lambda *refs: product_kernel(scale, *refs),
        grid=(1,),
        out_shape=[jax.ShapeDtypeStruct(shape, kind) for kind in (jnp.float32,) + (jnp.bfloat16,) * 3],
        in_specs=[pl.BlockSpec(memory_space=pltpu.SMEM)]
        + [pl.BlockSpec((rows, v.shape[1]), lambda i: (k, 0)) for v in parts[:-1]]
        + [pl.BlockSpec(v.shape, lambda i: (0, 0)) for v in (parts[-1], mine, other)],
        out_specs=[pl.BlockSpec(shape, lambda i: (0, 0, 0))] * 4,
        scratch_shapes=[pltpu.VMEM((2 * rows, mine.shape[1]), jnp.bfloat16)],
        compiler_params=pltpu.CompilerParams(vmem_limit_bytes=VMEM),
        cost_estimate=pl.CostEstimate(flops=1, bytes_accessed=1, transcendentals=0),
    )(flags, *parts, mine, other)


def arranged_kernel(flags, own, one, two, three, out):
    inner = flags[INNER] == 1
    second, third = jnp.where(inner, three[...], two[...]), jnp.where(inner, two[...], three[...])
    wide = own.shape[1]
    for slot, v in enumerate((own[...], one[...], second, third)):
        if out.ndim == 3:
            out[slot] = v
        else:
            out[:, slot * wide : (slot + 1) * wide] = v


def arranged(flags, got, stacked):
    rows, wide = got[0].shape
    vmem = pl.BlockSpec(memory_space=pltpu.VMEM)
    return pl.pallas_call(
        arranged_kernel,
        out_shape=jax.ShapeDtypeStruct((4, rows, wide) if stacked else (rows, 4 * wide), got[0].dtype),
        in_specs=[pl.BlockSpec(memory_space=pltpu.SMEM)] + [vmem] * 4,
        out_specs=vmem,
        compiler_params=pltpu.CompilerParams(vmem_limit_bytes=VMEM),
        cost_estimate=pl.CostEstimate(flops=1, bytes_accessed=1, transcendentals=0),
    )(flags, *got)


def fill_steering(steer, cos_c, sin_c, cos_f, sin_f, first, count):
    for i in range(count):
        cc, sc = cos_c[pl.ds(first + i, 1), :], sin_c[pl.ds(first + i, 1), :]
        steer[i * FINE : (i + 1) * FINE, :] = (cc * cos_f[...] - sc * sin_f[...]).astype(steer.dtype)
        steer[(count + i) * FINE : (count + i + 1) * FINE, :] = (sc * cos_f[...] + cc * sin_f[...]).astype(
            steer.dtype
        )


def conjugated(steer, spectra):
    found = nt(steer[...], spectra[...])
    rows, half = found.shape[0] // 2, found.shape[1] // 2
    return found[:rows, :half] + found[rows:, half:], found[rows:, :half] - found[:rows, half:]


def receivers_kernel(flags, *refs):
    tables, own, own_last, (given, other) = (refs[:4], refs[4:8]), refs[8:10], refs[10:12], refs[12:14]
    outs, (steer, spectra, steer_last, spectra_last) = refs[14:-4], refs[-4:]
    step = pl.program_id(0)

    @pl.when(step == 0)
    def _():
        first = 0
        for to, here in ((spectra, own), (spectra_last, own_last)):
            b_block, count = here[0].shape[2], here[0].shape[1] // 2
            to[: 2 * count, :b_block] = here[0][0]
            to[2 * count :, :b_block] = here[1][0]
            for t in range(2):
                rows = slice(first + t * count, first + (t + 1) * count)
                for part, place in ((given, flags[CORE]), (other, 1 - flags[CORE])):
                    at = pl.multiple_of((2 * t + place) * count, count)
                    to[pl.ds(at, count), b_block:] = part[rows, :]
            first += 2 * count

    coarse = tables[0][0].shape[0]
    fill_steering(steer, *tables[0], 0, coarse)
    real, imag = conjugated(steer, spectra)
    coarse_last = tables[1][0].shape[0] // len(outs)
    fill_steering(steer_last, *tables[1], step * coarse_last, coarse_last)
    real_last, imag_last = conjugated(steer_last, spectra_last)
    rows, wide = real.shape
    half, part = real_last.shape[0] // 2, wide // 2
    for k, out in enumerate(outs):

        @pl.when(step == k)
        def _(out=out):
            out[:rows, :wide] = real.astype(out.dtype)
            out[:rows, wide:] = imag.astype(out.dtype)
            for i in range(2):
                at = slice(i * half, (i + 1) * half)
                out[rows:, 2 * i * part : (2 * i + 1) * part] = real_last[at].astype(out.dtype)
                out[rows:, (2 * i + 1) * part : (2 * i + 2) * part] = imag_last[at].astype(out.dtype)


def receivers_of(flags, table, table_last, real, imag, given, other):
    planes = 4
    bins, wide, b_block = real.shape
    coarse, depth = table[0].shape
    rows, rows_last = coarse * FINE // planes, table_last[0].shape[0] * FINE // planes
    shape = jax.ShapeDtypeStruct((rows + rows_last // 2, 2 * wide), jnp.bfloat16)
    whole = lambda v: pl.BlockSpec(v.shape, lambda i, f: (0, 0))
    return pl.pallas_call(
        receivers_kernel,
        grid_spec=pltpu.PrefetchScalarGridSpec(
            num_scalar_prefetch=1,
            grid=(planes,),
            in_specs=[pl.BlockSpec((coarse // planes, depth), lambda i, f: (i, 0))] * 2
            + [whole(v) for v in (*table[2:], *table_last)]
            + [pl.BlockSpec((1, wide, b_block), lambda i, f: (f[MINE], 0, 0))] * 2
            + [pl.BlockSpec((1, wide // 2, b_block), lambda i, f: (bins - 1, f[PLACE_X], 0))] * 2
            + [whole(given), whole(other)],
            out_specs=[pl.BlockSpec(shape.shape, lambda i, f: (0, 0))] * planes,
            scratch_shapes=[
                pltpu.VMEM((2 * rows, depth), jnp.bfloat16),
                pltpu.VMEM((2 * wide, depth), jnp.bfloat16),
                pltpu.VMEM((2 * rows_last, depth), jnp.bfloat16),
                pltpu.VMEM((wide, depth), jnp.bfloat16),
            ],
        ),
        out_shape=[shape] * planes,
        compiler_params=pltpu.CompilerParams(vmem_limit_bytes=VMEM),
        cost_estimate=pl.CostEstimate(flops=1, bytes_accessed=1, transcendentals=0),
    )(flags, *table, *table_last, real, imag, real, imag, given, other)


def parted_kernel(flags, own, one, two, three, out, out_last):
    inner = flags[INNER] == 1
    second, third = jnp.where(inner, three[...], two[...]), jnp.where(inner, two[...], three[...])
    wide, half, rows = own.shape[1], own.shape[1] // 2, out.shape[0]
    rest = own.shape[0] - rows
    for slot, v in enumerate((own[...], one[...], second, third)):
        out[:, slot * wide : (slot + 1) * wide] = v[:rows]
        for i in range(2):
            out_last[i * rest : (i + 1) * rest, slot * half : (slot + 1) * half] = v[rows:, i * half : (i + 1) * half]


def parted(flags, got, rows):
    vmem = pl.BlockSpec(memory_space=pltpu.VMEM)
    high, wide = got[0].shape
    return pl.pallas_call(
        parted_kernel,
        out_shape=[
            jax.ShapeDtypeStruct((rows, 4 * wide), jnp.bfloat16),
            jax.ShapeDtypeStruct((2 * (high - rows), 2 * wide), jnp.bfloat16),
        ],
        in_specs=[pl.BlockSpec(memory_space=pltpu.SMEM)] + [vmem] * 4,
        out_specs=[vmem] * 2,
        compiler_params=pltpu.CompilerParams(vmem_limit_bytes=VMEM),
        cost_estimate=pl.CostEstimate(flops=1, bytes_accessed=1, transcendentals=0),
    )(flags, *got)


def place_kernel(flags, *refs):
    out, found = refs[-1], refs[-5:-1]
    for d, part in enumerate(found):

        @pl.when(pl.program_id(0) == d)
        def _(part=part):
            out[:, 0] = part[...].astype(out.dtype)


def placed(flags, whole, shape, found, k):
    rows = found[0].shape[0]
    before = [] if whole is None else [whole]
    return pl.pallas_call(
        place_kernel,
        grid_spec=pltpu.PrefetchScalarGridSpec(
            num_scalar_prefetch=1,
            grid=(4,),
            in_specs=[pl.BlockSpec(memory_space=pl.ANY)] * len(before)
            + [pl.BlockSpec(v.shape, lambda d, f: (0, 0, 0)) for v in found],
            out_specs=pl.BlockSpec((rows, 1) + shape[2:], lambda d, f: (k, f[MINE] ^ d, 0, 0)),
        ),
        out_shape=jax.ShapeDtypeStruct(shape, jnp.float32),
        input_output_aliases={1: 0} if before else {},
        compiler_params=pltpu.CompilerParams(vmem_limit_bytes=VMEM),
        cost_estimate=pl.CostEstimate(flops=1, bytes_accessed=1, transcendentals=0),
    )(flags, *before, *found)


def place_last_kernel(_, kept, given, out):
    out[:, 0] = kept[...] + given[...].astype(jnp.float32)


def placed_last(whole, kept, given):
    last = whole.shape[1] - 1
    block = pl.BlockSpec(given.shape, lambda i: (0, 0, 0))
    return pl.pallas_call(
        place_last_kernel,
        grid=(1,),
        in_specs=[pl.BlockSpec(memory_space=pl.ANY)] + [block] * 2,
        out_specs=pl.BlockSpec((given.shape[0], 1) + given.shape[1:], lambda i: (0, last, 0, 0)),
        out_shape=jax.ShapeDtypeStruct(whole.shape, jnp.float32),
        input_output_aliases={0: 0},
        compiler_params=pltpu.CompilerParams(vmem_limit_bytes=VMEM),
        cost_estimate=pl.CostEstimate(flops=1, bytes_accessed=1, transcendentals=0),
    )(whole, kept, given)


def shards_plane(src_real, src_imag, rcv_real, rcv_imag, src_pos, rcv_pos, freqs):
    n_z = lax.axis_size("tm")
    bins, wide, a_block = src_real.shape
    b_block = rcv_real.shape[2]
    half = wide // 2
    p_block = SRC_SL // lax.axis_size("src")
    q_plane = RCV_SL // n_z
    q_block = q_plane // 2
    q_sub = q_block // lax.axis_size("src")
    z, s, y = (lax.axis_index(name) for name in ("tm", "src", "rcv"))
    x, c = s // 2, s % 2
    mine = 2 * x + y
    last = bins - 1
    core = lambda v: lax.ppermute(v, "src", [(i, i ^ 1) for i in range(4)])
    over_x = lambda v: lax.ppermute(v, "src", [(i, i ^ 2) for i in range(4)])
    over_y = lambda v: lax.ppermute(v, "rcv", [(0, 1), (1, 0)])
    over_xy = lambda v: lax.ppermute(v, ("src", "rcv"), [(i, i ^ 5) for i in range(8)])
    over_z = lambda v, d: lax.ppermute(v, "tm", [(i, i ^ d) for i in range(n_z)])
    ends = lambda v: lax.ppermute(v, "tm", [(1, 0), (2, 3)])
    middle = lambda v: lax.ppermute(v, "tm", [(1, 2), (2, 1)])
    flat = lambda v: v.reshape(-1, v.shape[-1])
    take = lambda v, block, size: lax.dynamic_slice_in_dim(v, block * size, size)
    turn = [freqs]

    def after(v, *others):
        return lax.optimization_barrier((v, others))[0]

    def step(v):
        v = after(v, turn[0])
        turn[0] = v
        return v

    def bin_of(real, imag, which):
        return flat(jnp.stack([lax.dynamic_index_in_dim(part, which, 0, False) for part in (real, imag)]))

    def rows_of(which, first, count):
        at, size = (which, first, 0), (1, count, b_block)
        return jnp.concatenate([lax.dynamic_slice(v, at, size)[0] for v in (rcv_real, rcv_imag)], 0)

    spread = lambda got: [got[0]] + [over_z(got[d], d) for d in range(1, n_z)]
    inner = (z == 1) | (z == 2)
    flags = jnp.stack([v.astype(jnp.int32) for v in (y, c, inner, c == y, mine, x)])

    x_given = over_x(step(bin_of(src_real, src_imag, 2 * (1 - x) + y)))
    y_given = [rows_of(2 * x + 1 - y, c * half, half), rows_of(last, x * half + c * (half // 2), half // 2)]
    y_given = over_y(step(jnp.concatenate(y_given, 0)))
    raw = lax.dynamic_slice_in_dim(jnp.stack([src_real[last], src_imag[last]]), y * half, half, 1)
    raw = spread([step(flat(raw))] * n_z)
    x_own = step(bin_of(src_real, src_imag, mine))
    raw[1], x_own = step((raw[1], x_own))
    x_other = core(x_own)

    at_src = jnp.concatenate([take(src_pos, block, a_block) for block in (s, s ^ 2, s ^ 1, s ^ 3)])
    at_rcv = jnp.concatenate([take(rcv_pos, block, b_block) for block in (y, 1 - y)])
    f_mine, f_last = lax.dynamic_index_in_dim(freqs, mine, 0, False), freqs[last]
    here, there = s * p_block, (s ^ 2) * p_block
    cuts = [cut * p_block // CUTS[-1] for cut in CUTS]
    spans = list(zip(cuts, cuts[1:]))
    runs = [(i, n) for span in spans for i in range(2) for n in range(*span, FINE)]
    side, first = jnp.array([i for i, _ in runs], jnp.int32), jnp.array([n for _, n in runs], jnp.int32)
    starts = jnp.where(side == 0, here, there) + first
    t_source = step(tables(f_mine, starts, SRC_SL, at_src))
    x_given = step(x_given)
    x_cross = core(x_given)
    n = jnp.arange(n_z * q_block // FINE, dtype=jnp.int32) * FINE
    t_receiver = tables(f_mine, (z ^ n // q_block) * q_plane + c * q_block + n % q_block, RCV_SL, at_rcv)
    q_half = q_block // 2
    n = jnp.arange(n_z * q_half // FINE, dtype=jnp.int32) * FINE
    starts = (z ^ n // q_half) * q_plane + y * q_block + c * q_half + n % q_half
    t_receiver_last = tables(f_last, starts, RCV_SL, at_rcv)
    t_receiver, t_receiver_last = step((t_receiver, t_receiver_last))
    y_given = step(y_given)
    y_other = core(y_given)
    x_cross, x_other, raw = step((x_cross, x_other, raw))
    raw = step(arranged(flags, raw, True))
    other_raw = over_y(raw)
    pieces = step(steered(flags, t_source, [x_own, x_given, x_other, x_cross], 4, joined=True))
    near, one = over_z(pieces, 1), middle(pieces)
    y_other = step(y_other)
    yr = receivers_of(flags, t_receiver, t_receiver_last, rcv_real, rcv_imag, y_given, y_other)
    yr, other_raw = step((yr, other_raw))
    yr = spread(yr)
    near, one, yr = step((near, one, yr))

    two, three = middle(near), ends(one)
    yr_mine, yr_last = step(parted(flags, yr, q_block))
    yr_other = core(yr_mine)
    yr_last = lax.all_gather(yr_last, "src", axis=0)
    focus_scale = 1.0 / float(wide * n_z * RCV_ST) ** 0.5
    beam_scale = 1.0 / float(SRC_ST) ** 0.5
    f_last = after(f_last, yr_mine)
    n = jnp.arange(2 * p_block // FINE, dtype=jnp.int32) * FINE
    starts = jnp.where(n < p_block, here, there) + n % p_block
    at_cores = jnp.concatenate([take(src_pos, block, a_block) for block in (s, s ^ 1)])
    t_source_last = tables(f_last, starts, SRC_SL, at_cores)
    yr_last, t_source_last = step((yr_last, t_source_last))
    focus = step(focused(focus_scale, flags, raw, other_raw, yr_last))
    focus = step([focus, core(focus)])
    two, three, yr_other = step((two, three, yr_other))
    four = [ends(two[2 * first : 2 * past]) for first, past in spans]
    kept, given = step(steered(flags, t_source_last, focus, 2, scale=beam_scale, paired=True))
    given = over_x(given)
    shape = (p_block, bins, 2, q_block)
    parts = [pieces, near, one, three, two]
    scale = focus_scale * beam_scale
    sent, whole = [], None
    for k, (first, past) in enumerate(spans):
        rows = 2 * (past - first)
        four[k] = step(four[k])
        found = step(product(scale, 2 * first // rows, rows, flags, [*parts, four[k]], yr_mine, yr_other))
        if k == 0:
            given = step(given)
        if k > 0:
            sent[-1] = step(sent[-1])
        sent.append([found[0], over_y(found[1]), over_x(found[2]), over_xy(found[3])])
    for k, (first, past) in enumerate(spans):
        found = step(sent[k]) if k == len(spans) - 1 else sent[k]
        whole = placed(flags, whole, shape, found, first // (past - first))
        if k == 0:
            whole = placed_last(whole, kept, given)
    return whole.transpose(0, 2, 1, 3)


def solution(mesh):
    plane = (mesh.shape["tm"], mesh.shape["src"], mesh.shape["rcv"]) == (4, 4, 2)
    shards = shards_plane if plane else shards_any
    in_specs = (
        P(None, "tm", "src"),
        P(None, "tm", "src"),
        P(None, "tm", "rcv"),
        P(None, "tm", "rcv"),
        P(),
        P(),
        P(),
    )
    out_specs = P("src", None, None, ("tm", "rcv"))
    return jax.shard_map(shards, mesh=mesh, in_specs=in_specs, out_specs=out_specs, check_vma=False)
```

```python
import jax
import jax.numpy as jnp
from jax import lax
from jax.experimental import pallas as pl
from jax.experimental.pallas import tpu as pltpu
from jax.sharding import PartitionSpec as P

SRC_ST = 2048
RCV_ST = 2048
SRC_SL = 2048
RCV_SL = 2048


TWO_PI = 6.283185307179586


def grid_points(first, count, total):
    index = (first + jnp.arange(count, dtype=jnp.int32)).astype(jnp.float32)
    return (2.0 * index + 1.0) / total - 1.0


def phases(freqs, slowness, positions):
    return (TWO_PI * freqs)[:, None, None] * slowness[None, :, None] * positions[None, None, :]


def mixed(form, first, second):
    return jnp.einsum(form, first, second, preferred_element_type=jnp.float32)


def receiver_fold(freqs, slow_rcv, locate, piece, start):
    part_real, part_imag = piece
    where = locate(start, part_real.shape[2])
    angle = phases(freqs, slow_rcv, where)
    steer_real = jnp.cos(angle).astype(jnp.bfloat16)
    steer_imag = jnp.sin(angle).astype(jnp.bfloat16)
    new_real = mixed("fab,fqb->faq", part_real, steer_real) - mixed(
        "fab,fqb->faq", part_imag, steer_imag
    )
    new_imag = mixed("fab,fqb->faq", part_real, steer_imag) + mixed(
        "fab,fqb->faq", part_imag, steer_real
    )
    return (new_real, new_imag)


def source_terms(freqs, slow_src, positions, focus_real, focus_imag):
    angle = phases(freqs, slow_src, positions)
    steer_real = jnp.cos(angle).astype(jnp.bfloat16)
    steer_imag = (-jnp.sin(angle)).astype(jnp.bfloat16)
    term_real = mixed("fpa,faq->pfq", steer_real, focus_real) - mixed(
        "fpa,faq->pfq", steer_imag, focus_imag
    )
    term_imag = mixed("fpa,faq->pfq", steer_real, focus_imag) + mixed(
        "fpa,faq->pfq", steer_imag, focus_real
    )
    return (term_real, term_imag)


def shards_any(src_real, src_imag, rcv_real, rcv_imag, src_pos, rcv_pos, freqs):
    n_time = lax.axis_size("tm")
    n_recv = lax.axis_size("rcv")
    n_source = lax.axis_size("src")
    src_block = src_real.shape[2]
    rcv_block = rcv_real.shape[2]
    windows = src_real.shape[1] * n_time
    q_block = RCV_SL // (n_time * n_recv)
    p_block = SRC_SL // n_source
    src_both = jnp.concatenate([src_real, src_imag], 1)
    rcv_plain = jnp.concatenate([rcv_real, rcv_imag], 1)
    rcv_turned = jnp.concatenate([-rcv_imag, rcv_real], 1)
    part_real = mixed("fwa,fwb->fab", src_both, rcv_plain)
    part_imag = mixed("fwa,fwb->fab", src_both, rcv_turned)
    q_first = (lax.axis_index("tm") * n_recv + lax.axis_index("rcv")) * q_block
    slow_rcv = grid_points(q_first, q_block, RCV_SL)
    sum_real, sum_imag = (
        lax.psum_scatter(part_real, "tm", scatter_dimension=2, tiled=True),
        lax.psum_scatter(part_imag, "tm", scatter_dimension=2, tiled=True),
    )
    sub_width = rcv_block // n_time

    def mapped(start, count):
        column = jnp.arange(count, dtype=jnp.int32)
        block = column // sub_width
        natural = block % n_recv * rcv_block + block // n_recv * sub_width + column % sub_width
        return jnp.take(rcv_pos, natural)

    cross = (sum_real.astype(jnp.bfloat16), sum_imag.astype(jnp.bfloat16))
    focus_real, focus_imag = receiver_fold(
        freqs,
        slow_rcv,
        mapped,
        (
            lax.all_gather(cross[0], ("tm", "rcv"), axis=2, tiled=True),
            lax.all_gather(cross[1], ("tm", "rcv"), axis=2, tiled=True),
        ),
        jnp.int32(0),
    )
    focus_scale = 1.0 / jnp.sqrt(jnp.float32(windows * RCV_ST))
    focus_real = (focus_real * focus_scale).astype(jnp.bfloat16)
    focus_imag = (focus_imag * focus_scale).astype(jnp.bfloat16)
    beam_scale = 1.0 / jnp.sqrt(jnp.float32(SRC_ST))
    own_pos = lax.dynamic_slice_in_dim(src_pos, lax.axis_index("src") * src_block, src_block)
    slow_src = grid_points(jnp.int32(0), p_block * lax.axis_size("src"), SRC_SL)
    term_real, term_imag = source_terms(freqs, slow_src, own_pos, focus_real, focus_imag)
    return lax.psum_scatter(
        jnp.stack([term_real, term_imag], 1) * beam_scale, "src", scatter_dimension=0, tiled=True
    )


FINE = 32
CUTS = (0, 3, 6, 8)
PLACE_Y, CORE, INNER, SAME, MINE, PLACE_X = range(6)
VMEM = 48 * 1024 * 1024


def waves(freq, slowness, positions):
    angle = ((TWO_PI * freq) * slowness)[:, None] * positions[None, :]
    return jnp.cos(angle), jnp.sin(angle)


def tables(freq, starts, total, positions):
    coarse = (2.0 * starts.astype(jnp.float32) + 1.0) / total - 1.0
    fine = 2.0 * jnp.arange(FINE, dtype=jnp.float32) / total
    return waves(freq, coarse, positions) + waves(freq, fine, positions)


def nt(first, second):
    return lax.dot_general(first, second, (((1,), (1,)), ((), ())), preferred_element_type=jnp.float32)


def steered_kernel(sign, scale, n_parts, n_halves, flags, cos_c, sin_c, cos_f, sin_f, *refs):
    parts, halves = refs[:n_parts], refs[n_parts : n_parts + n_halves]
    outs, (steer, spectra) = refs[n_parts + n_halves : -2], refs[-2:]
    step = pl.program_id(0)
    group = cos_c.shape[0]
    rows = group * FINE

    @pl.when(step == 0)
    def _():
        first = 0
        for part in parts:
            spectra[:, first : first + part.shape[1]] = part[...]
            first += part.shape[1]
        for i, part in enumerate(halves):
            count = part.shape[0] // 2
            for t in range(2):
                at = 2 * t * count + (flags[CORE] if i == 0 else 1 - flags[CORE]) * count
                spectra[pl.ds(pl.multiple_of(at, count), count), first:] = part[t * count : (t + 1) * count, :]

    for i in range(group):
        cc, sc = cos_c[i : i + 1, :], sin_c[i : i + 1, :]
        steer[i * FINE : (i + 1) * FINE, :] = (cc * cos_f[...] - sc * sin_f[...]).astype(jnp.bfloat16)
        steer[rows + i * FINE : rows + (i + 1) * FINE, :] = (sc * cos_f[...] + cc * sin_f[...]).astype(
            jnp.bfloat16
        )
    found = nt(steer[...], spectra[...])
    half = found.shape[1] // 2
    real = (found[:rows, :half] + found[rows:, half:]) * scale
    imag = (found[:rows, half:] - found[rows:, :half]) * (sign * scale)
    for k, out in enumerate(outs):

        size = out.shape[0]
        per = rows // size

        @pl.when((step == k // per) | (len(outs) == 1))
        def _(out=out, at=k % per * size):
            if out.ndim == 2:
                out[:, :half] = real[at : at + size].astype(out.dtype)
                out[:, half:] = imag[at : at + size].astype(out.dtype)
            else:
                out[:, 0, :] = real.astype(out.dtype)
                out[:, 1, :] = imag.astype(out.dtype)


def steered(flags, table, parts, steps, halves=(), cuts=1, sign=1.0, scale=1.0, paired=False, joined=False):
    coarse, depth = table[0].shape
    wide = parts[0].shape[0]
    group = coarse // steps
    rows = group * FINE
    whole = lambda v: pl.BlockSpec(v.shape, lambda i: (0, 0))
    if paired:
        shape, spec = jax.ShapeDtypeStruct((rows, 2, wide // 2), jnp.float32), pl.BlockSpec(
            (rows, 2, wide // 2), lambda i: (0, 0, 0)
        )
    else:
        shape, spec = jax.ShapeDtypeStruct((rows, wide), jnp.bfloat16), pl.BlockSpec((rows, wide), lambda i: (0, 0))
    shapes, specs = [shape] * steps, [spec] * steps
    if paired:
        shapes[1:] = [jax.ShapeDtypeStruct(shape.shape, jnp.bfloat16)] * (steps - 1)
    if cuts > 1:
        shapes = [jax.ShapeDtypeStruct((rows // cuts, wide), jnp.bfloat16)] * (steps * cuts)
        specs = [pl.BlockSpec((rows // cuts, wide), lambda i: (0, 0))] * (steps * cuts)
    if joined:
        shapes = jax.ShapeDtypeStruct((steps * rows, wide), jnp.bfloat16)
        specs = pl.BlockSpec((rows, wide), lambda i: (i, 0))
    return pl.pallas_call(
        lambda *refs: steered_kernel(sign, scale, len(parts), len(halves), *refs),
        grid=(steps,),
        in_specs=[pl.BlockSpec(memory_space=pltpu.SMEM)]
        + [pl.BlockSpec((group, depth), lambda i: (i, 0))] * 2
        + [whole(v) for v in (*table[2:], *parts, *halves)],
        out_specs=specs,
        out_shape=shapes,
        scratch_shapes=[pltpu.VMEM((2 * rows, depth), jnp.bfloat16), pltpu.VMEM((wide, depth), jnp.bfloat16)],
        compiler_params=pltpu.CompilerParams(vmem_limit_bytes=VMEM),
        cost_estimate=pl.CostEstimate(flops=1, bytes_accessed=1, transcendentals=0),
    )(flags, *table, *parts, *halves)


def focus_kernel(scale, flags, slots, others, receiver, out, real, imag, both):
    n_z, rows, _ = slots.shape
    half = rows // 2
    wide = rows
    part = receiver.shape[1]
    q = 2 * part
    for slot in range(n_z):
        for v, at in ((slots, flags[PLACE_Y] * half), (others, (1 - flags[PLACE_Y]) * half)):
            to = pl.ds(pl.multiple_of(slot * wide + at, half), half)
            real[to, :] = v[slot, :half, :]
            imag[to, :] = v[slot, half:, :]
        for t in range(2):
            for i in range(receiver.shape[0]):
                row, col = t * q + i % 2 * part, slot * wide + i // 2 * half
                both[row : row + part, col : col + half] = receiver[i, :, (2 * slot + t) * half : (2 * slot + t + 1) * half]
    one = jnp.dot(both[...], real[...], preferred_element_type=jnp.float32)
    two = jnp.dot(both[...], imag[...], preferred_element_type=jnp.float32)
    out[:q, :] = ((one[:q] - two[q:]) * scale).astype(out.dtype)
    out[q:, :] = ((one[q:] + two[:q]) * scale).astype(out.dtype)


def focused(scale, flags, slots, others, receiver):
    n_z, rows, stations = slots.shape
    q = 2 * receiver.shape[1]
    return pl.pallas_call(
        lambda *refs: focus_kernel(scale, *refs),
        out_shape=jax.ShapeDtypeStruct((2 * q, stations), jnp.bfloat16),
        grid=(1,),
        in_specs=[pl.BlockSpec(memory_space=pltpu.SMEM)]
        + [pl.BlockSpec(v.shape, lambda i: (0, 0, 0)) for v in (slots, others, receiver)],
        out_specs=pl.BlockSpec((2 * q, stations), lambda i: (0, 0)),
        scratch_shapes=[pltpu.VMEM((n_z * rows, stations), jnp.bfloat16)] * 2
        + [pltpu.VMEM((2 * q, n_z * rows), jnp.bfloat16)],
        compiler_params=pltpu.CompilerParams(vmem_limit_bytes=VMEM),
        cost_estimate=pl.CostEstimate(flops=1, bytes_accessed=1, transcendentals=0),
    )(flags, slots, others, receiver)


def product_kernel(scale, flags, own, near, one, two, three, four, mine, other, *refs):
    outs, both = refs[:-1], refs[-1]
    rows = both.shape[0] // 2
    wide = own.shape[1]
    half = wide // 2
    for slot, part in enumerate((own[...], near[...], one[...] + two[...], three[...] + four[...])):
        at = slot * wide
        real, imag = part[:, :half], part[:, half:]
        both[:rows, at : at + half] = real
        both[:rows, at + half : at + wide] = -imag
        both[rows:, at : at + half] = imag
        both[rows:, at + half : at + wide] = real
    middle = rows // 2
    same = flags[SAME] == 1
    by_mine, by_other = nt(both[...], mine[...]) * scale, nt(both[...], other[...]) * scale
    for total, one, two in (
        (jnp.where(same, by_mine, by_other), outs[0], outs[2]),
        (jnp.where(same, by_other, by_mine), outs[1], outs[3]),
    ):
        for t in range(2):
            one[:, t, :] = total[t * rows : t * rows + middle].astype(one.dtype)
            two[:, t, :] = total[t * rows + middle : (t + 1) * rows].astype(two.dtype)


def product(scale, k, rows, flags, parts, mine, other):
    shape = (rows // 2, 2, mine.shape[0])
    return pl.pallas_call(
        lambda *refs: product_kernel(scale, *refs),
        grid=(1,),
        out_shape=[jax.ShapeDtypeStruct(shape, kind) for kind in (jnp.float32,) + (jnp.bfloat16,) * 3],
        in_specs=[pl.BlockSpec(memory_space=pltpu.SMEM)]
        + [pl.BlockSpec((rows, v.shape[1]), lambda i: (k, 0)) for v in parts[:-1]]
        + [pl.BlockSpec(v.shape, lambda i: (0, 0)) for v in (parts[-1], mine, other)],
        out_specs=[pl.BlockSpec(shape, lambda i: (0, 0, 0))] * 4,
        scratch_shapes=[pltpu.VMEM((2 * rows, mine.shape[1]), jnp.bfloat16)],
        compiler_params=pltpu.CompilerParams(vmem_limit_bytes=VMEM),
        cost_estimate=pl.CostEstimate(flops=1, bytes_accessed=1, transcendentals=0),
    )(flags, *parts, mine, other)


def arranged_kernel(flags, own, one, two, three, out):
    inner = flags[INNER] == 1
    second, third = jnp.where(inner, three[...], two[...]), jnp.where(inner, two[...], three[...])
    wide = own.shape[1]
    for slot, v in enumerate((own[...], one[...], second, third)):
        if out.ndim == 3:
            out[slot] = v
        else:
            out[:, slot * wide : (slot + 1) * wide] = v


def arranged(flags, got, stacked):
    rows, wide = got[0].shape
    vmem = pl.BlockSpec(memory_space=pltpu.VMEM)
    return pl.pallas_call(
        arranged_kernel,
        out_shape=jax.ShapeDtypeStruct((4, rows, wide) if stacked else (rows, 4 * wide), got[0].dtype),
        in_specs=[pl.BlockSpec(memory_space=pltpu.SMEM)] + [vmem] * 4,
        out_specs=vmem,
        compiler_params=pltpu.CompilerParams(vmem_limit_bytes=VMEM),
        cost_estimate=pl.CostEstimate(flops=1, bytes_accessed=1, transcendentals=0),
    )(flags, *got)


def fill_steering(steer, cos_c, sin_c, cos_f, sin_f, first, count):
    for i in range(count):
        cc, sc = cos_c[pl.ds(first + i, 1), :], sin_c[pl.ds(first + i, 1), :]
        steer[i * FINE : (i + 1) * FINE, :] = (cc * cos_f[...] - sc * sin_f[...]).astype(steer.dtype)
        steer[(count + i) * FINE : (count + i + 1) * FINE, :] = (sc * cos_f[...] + cc * sin_f[...]).astype(
            steer.dtype
        )


def conjugated(steer, spectra):
    found = nt(steer[...], spectra[...])
    rows, half = found.shape[0] // 2, found.shape[1] // 2
    return found[:rows, :half] + found[rows:, half:], found[rows:, :half] - found[:rows, half:]


def receivers_kernel(flags, *refs):
    tables, own, own_last, (given, other) = (refs[:4], refs[4:8]), refs[8:10], refs[10:12], refs[12:14]
    outs, (steer, spectra, steer_last, spectra_last) = refs[14:-4], refs[-4:]
    step = pl.program_id(0)

    @pl.when(step == 0)
    def _():
        first = 0
        for to, here in ((spectra, own), (spectra_last, own_last)):
            b_block, count = here[0].shape[2], here[0].shape[1] // 2
            to[: 2 * count, :b_block] = here[0][0]
            to[2 * count :, :b_block] = here[1][0]
            for t in range(2):
                rows = slice(first + t * count, first + (t + 1) * count)
                for part, place in ((given, flags[CORE]), (other, 1 - flags[CORE])):
                    at = pl.multiple_of((2 * t + place) * count, count)
                    to[pl.ds(at, count), b_block:] = part[rows, :]
            first += 2 * count

    coarse = tables[0][0].shape[0]
    fill_steering(steer, *tables[0], 0, coarse)
    real, imag = conjugated(steer, spectra)
    coarse_last = tables[1][0].shape[0] // len(outs)
    fill_steering(steer_last, *tables[1], step * coarse_last, coarse_last)
    real_last, imag_last = conjugated(steer_last, spectra_last)
    rows, wide = real.shape
    half, part = real_last.shape[0] // 2, wide // 2
    for k, out in enumerate(outs):

        @pl.when(step == k)
        def _(out=out):
            out[:rows, :wide] = real.astype(out.dtype)
            out[:rows, wide:] = imag.astype(out.dtype)
            for i in range(2):
                at = slice(i * half, (i + 1) * half)
                out[rows:, 2 * i * part : (2 * i + 1) * part] = real_last[at].astype(out.dtype)
                out[rows:, (2 * i + 1) * part : (2 * i + 2) * part] = imag_last[at].astype(out.dtype)


def receivers_of(flags, table, table_last, real, imag, given, other):
    planes = 4
    bins, wide, b_block = real.shape
    coarse, depth = table[0].shape
    rows, rows_last = coarse * FINE // planes, table_last[0].shape[0] * FINE // planes
    shape = jax.ShapeDtypeStruct((rows + rows_last // 2, 2 * wide), jnp.bfloat16)
    whole = lambda v: pl.BlockSpec(v.shape, lambda i, f: (0, 0))
    return pl.pallas_call(
        receivers_kernel,
        grid_spec=pltpu.PrefetchScalarGridSpec(
            num_scalar_prefetch=1,
            grid=(planes,),
            in_specs=[pl.BlockSpec((coarse // planes, depth), lambda i, f: (i, 0))] * 2
            + [whole(v) for v in (*table[2:], *table_last)]
            + [pl.BlockSpec((1, wide, b_block), lambda i, f: (f[MINE], 0, 0))] * 2
            + [pl.BlockSpec((1, wide // 2, b_block), lambda i, f: (bins - 1, f[PLACE_X], 0))] * 2
            + [whole(given), whole(other)],
            out_specs=[pl.BlockSpec(shape.shape, lambda i, f: (0, 0))] * planes,
            scratch_shapes=[
                pltpu.VMEM((2 * rows, depth), jnp.bfloat16),
                pltpu.VMEM((2 * wide, depth), jnp.bfloat16),
                pltpu.VMEM((2 * rows_last, depth), jnp.bfloat16),
                pltpu.VMEM((wide, depth), jnp.bfloat16),
            ],
        ),
        out_shape=[shape] * planes,
        compiler_params=pltpu.CompilerParams(vmem_limit_bytes=VMEM),
        cost_estimate=pl.CostEstimate(flops=1, bytes_accessed=1, transcendentals=0),
    )(flags, *table, *table_last, real, imag, real, imag, given, other)


def parted_kernel(flags, own, one, two, three, out, out_last):
    inner = flags[INNER] == 1
    second, third = jnp.where(inner, three[...], two[...]), jnp.where(inner, two[...], three[...])
    wide, half, rows = own.shape[1], own.shape[1] // 2, out.shape[0]
    rest = own.shape[0] - rows
    for slot, v in enumerate((own[...], one[...], second, third)):
        out[:, slot * wide : (slot + 1) * wide] = v[:rows]
        for i in range(2):
            out_last[i * rest : (i + 1) * rest, slot * half : (slot + 1) * half] = v[rows:, i * half : (i + 1) * half]


def parted(flags, got, rows):
    vmem = pl.BlockSpec(memory_space=pltpu.VMEM)
    high, wide = got[0].shape
    return pl.pallas_call(
        parted_kernel,
        out_shape=[
            jax.ShapeDtypeStruct((rows, 4 * wide), jnp.bfloat16),
            jax.ShapeDtypeStruct((2 * (high - rows), 2 * wide), jnp.bfloat16),
        ],
        in_specs=[pl.BlockSpec(memory_space=pltpu.SMEM)] + [vmem] * 4,
        out_specs=[vmem] * 2,
        compiler_params=pltpu.CompilerParams(vmem_limit_bytes=VMEM),
        cost_estimate=pl.CostEstimate(flops=1, bytes_accessed=1, transcendentals=0),
    )(flags, *got)


def place_kernel(flags, *refs):
    out, found = refs[-1], refs[-5:-1]
    for d, part in enumerate(found):

        @pl.when(pl.program_id(0) == d)
        def _(part=part):
            out[:, 0] = part[...].astype(out.dtype)


def placed(flags, whole, shape, found, k):
    rows = found[0].shape[0]
    before = [] if whole is None else [whole]
    return pl.pallas_call(
        place_kernel,
        grid_spec=pltpu.PrefetchScalarGridSpec(
            num_scalar_prefetch=1,
            grid=(4,),
            in_specs=[pl.BlockSpec(memory_space=pl.ANY)] * len(before)
            + [pl.BlockSpec(v.shape, lambda d, f: (0, 0, 0)) for v in found],
            out_specs=pl.BlockSpec((rows, 1) + shape[2:], lambda d, f: (k, f[MINE] ^ d, 0, 0)),
        ),
        out_shape=jax.ShapeDtypeStruct(shape, jnp.float32),
        input_output_aliases={1: 0} if before else {},
        compiler_params=pltpu.CompilerParams(vmem_limit_bytes=VMEM),
        cost_estimate=pl.CostEstimate(flops=1, bytes_accessed=1, transcendentals=0),
    )(flags, *before, *found)


def place_last_kernel(_, kept, given, out):
    out[:, 0] = kept[...] + given[...].astype(jnp.float32)


def placed_last(whole, kept, given):
    last = whole.shape[1] - 1
    block = pl.BlockSpec(given.shape, lambda i: (0, 0, 0))
    return pl.pallas_call(
        place_last_kernel,
        grid=(1,),
        in_specs=[pl.BlockSpec(memory_space=pl.ANY)] + [block] * 2,
        out_specs=pl.BlockSpec((given.shape[0], 1) + given.shape[1:], lambda i: (0, last, 0, 0)),
        out_shape=jax.ShapeDtypeStruct(whole.shape, jnp.float32),
        input_output_aliases={0: 0},
        compiler_params=pltpu.CompilerParams(vmem_limit_bytes=VMEM),
        cost_estimate=pl.CostEstimate(flops=1, bytes_accessed=1, transcendentals=0),
    )(whole, kept, given)


def shards_plane(src_real, src_imag, rcv_real, rcv_imag, src_pos, rcv_pos, freqs):
    n_z = lax.axis_size("tm")
    bins, wide, a_block = src_real.shape
    b_block = rcv_real.shape[2]
    half = wide // 2
    p_block = SRC_SL // lax.axis_size("src")
    q_plane = RCV_SL // n_z
    q_block = q_plane // 2
    q_sub = q_block // lax.axis_size("src")
    z, s, y = (lax.axis_index(name) for name in ("tm", "src", "rcv"))
    x, c = s // 2, s % 2
    mine = 2 * x + y
    last = bins - 1
    core = lambda v: lax.ppermute(v, "src", [(i, i ^ 1) for i in range(4)])
    over_x = lambda v: lax.ppermute(v, "src", [(i, i ^ 2) for i in range(4)])
    over_y = lambda v: lax.ppermute(v, "rcv", [(0, 1), (1, 0)])
    over_xy = lambda v: lax.ppermute(v, ("src", "rcv"), [(i, i ^ 5) for i in range(8)])
    over_z = lambda v, d: lax.ppermute(v, "tm", [(i, i ^ d) for i in range(n_z)])
    ends = lambda v: lax.ppermute(v, "tm", [(1, 0), (2, 3)])
    middle = lambda v: lax.ppermute(v, "tm", [(1, 2), (2, 1)])
    flat = lambda v: v.reshape(-1, v.shape[-1])
    take = lambda v, block, size: lax.dynamic_slice_in_dim(v, block * size, size)
    turn = [freqs]

    def after(v, *others):
        return lax.optimization_barrier((v, others))[0]

    def step(v):
        v = after(v, turn[0])
        turn[0] = v
        return v

    def bin_of(real, imag, which):
        return flat(jnp.stack([lax.dynamic_index_in_dim(part, which, 0, False) for part in (real, imag)]))

    def rows_of(which, first, count):
        at, size = (which, first, 0), (1, count, b_block)
        return jnp.concatenate([lax.dynamic_slice(v, at, size)[0] for v in (rcv_real, rcv_imag)], 0)

    spread = lambda got: [got[0]] + [over_z(got[d], d) for d in range(1, n_z)]
    inner = (z == 1) | (z == 2)
    flags = jnp.stack([v.astype(jnp.int32) for v in (y, c, inner, c == y, mine, x)])

    x_given = over_x(step(bin_of(src_real, src_imag, 2 * (1 - x) + y)))
    y_given = [rows_of(2 * x + 1 - y, c * half, half), rows_of(last, x * half + c * (half // 2), half // 2)]
    y_given = over_y(step(jnp.concatenate(y_given, 0)))
    raw = lax.dynamic_slice_in_dim(jnp.stack([src_real[last], src_imag[last]]), y * half, half, 1)
    raw = spread([step(flat(raw))] * n_z)
    x_own = step(bin_of(src_real, src_imag, mine))
    raw[1], x_own = step((raw[1], x_own))
    x_other = core(x_own)

    at_src = jnp.concatenate([take(src_pos, block, a_block) for block in (s, s ^ 2, s ^ 1, s ^ 3)])
    at_rcv = jnp.concatenate([take(rcv_pos, block, b_block) for block in (y, 1 - y)])
    f_mine, f_last = lax.dynamic_index_in_dim(freqs, mine, 0, False), freqs[last]
    here, there = s * p_block, (s ^ 2) * p_block
    cuts = [cut * p_block // CUTS[-1] for cut in CUTS]
    spans = list(zip(cuts, cuts[1:]))
    runs = [(i, n) for span in spans for i in range(2) for n in range(*span, FINE)]
    side, first = jnp.array([i for i, _ in runs], jnp.int32), jnp.array([n for _, n in runs], jnp.int32)
    starts = jnp.where(side == 0, here, there) + first
    t_source = step(tables(f_mine, starts, SRC_SL, at_src))
    x_given = step(x_given)
    x_cross = core(x_given)
    n = jnp.arange(n_z * q_block // FINE, dtype=jnp.int32) * FINE
    t_receiver = tables(f_mine, (z ^ n // q_block) * q_plane + c * q_block + n % q_block, RCV_SL, at_rcv)
    q_half = q_block // 2
    n = jnp.arange(n_z * q_half // FINE, dtype=jnp.int32) * FINE
    starts = (z ^ n // q_half) * q_plane + y * q_block + c * q_half + n % q_half
    t_receiver_last = tables(f_last, starts, RCV_SL, at_rcv)
    t_receiver, t_receiver_last = step((t_receiver, t_receiver_last))
    y_given = step(y_given)
    y_other = core(y_given)
    x_cross, x_other, raw = step((x_cross, x_other, raw))
    raw = step(arranged(flags, raw, True))
    other_raw = over_y(raw)
    pieces = step(steered(flags, t_source, [x_own, x_given, x_other, x_cross], 4, joined=True))
    near, one = over_z(pieces, 1), middle(pieces)
    y_other = step(y_other)
    yr = receivers_of(flags, t_receiver, t_receiver_last, rcv_real, rcv_imag, y_given, y_other)
    yr, other_raw = step((yr, other_raw))
    f_last = after(f_last, yr)
    n = jnp.arange(2 * p_block // FINE, dtype=jnp.int32) * FINE
    starts = jnp.where(n < p_block, here, there) + n % p_block
    at_cores = jnp.concatenate([take(src_pos, block, a_block) for block in (s, s ^ 1)])
    t_source_last = tables(f_last, starts, SRC_SL, at_cores)
    yr = spread(yr)
    near, one, yr, t_source_last = step((near, one, yr, t_source_last))

    two, three = middle(near), ends(one)
    yr_mine, yr_last = step(parted(flags, yr, q_block))
    yr_other = core(yr_mine)
    yr_last = lax.all_gather(yr_last, "src", axis=0)
    focus_scale = 1.0 / float(wide * n_z * RCV_ST) ** 0.5
    beam_scale = 1.0 / float(SRC_ST) ** 0.5
    yr_last = step(yr_last)
    focus = step(focused(focus_scale, flags, raw, other_raw, yr_last))
    focus = step([focus, core(focus)])
    two, three, yr_other = step((two, three, yr_other))
    four = [ends(two[2 * first : 2 * past]) for first, past in spans]
    kept, given = step(steered(flags, t_source_last, focus, 2, scale=beam_scale, paired=True))
    given = over_x(given)
    shape = (p_block, bins, 2, q_block)
    parts = [pieces, near, one, three, two]
    scale = focus_scale * beam_scale
    sent, whole = [], None
    for k, (first, past) in enumerate(spans):
        rows = 2 * (past - first)
        four[k] = step(four[k])
        found = step(product(scale, 2 * first // rows, rows, flags, [*parts, four[k]], yr_mine, yr_other))
        if k == 0:
            given = step(given)
        if k > 0:
            sent[-1] = step(sent[-1])
        sent.append([found[0], over_y(found[1]), over_x(found[2]), over_xy(found[3])])
    for k, (first, past) in enumerate(spans):
        found = step(sent[k]) if k == len(spans) - 1 else sent[k]
        whole = placed(flags, whole, shape, found, first // (past - first))
        if k == 0:
            whole = placed_last(whole, kept, given)
    return whole.transpose(0, 2, 1, 3)


def solution(mesh):
    plane = (mesh.shape["tm"], mesh.shape["src"], mesh.shape["rcv"]) == (4, 4, 2)
    shards = shards_plane if plane else shards_any
    in_specs = (
        P(None, "tm", "src"),
        P(None, "tm", "src"),
        P(None, "tm", "rcv"),
        P(None, "tm", "rcv"),
        P(),
        P(),
        P(),
    )
    out_specs = P("src", None, None, ("tm", "rcv"))
    return jax.shard_map(shards, mesh=mesh, in_specs=in_specs, out_specs=out_specs, check_vma=False)
```
